256 devices in a mesh: row: 8 (over x, core), col: 32 (over z, y).
Axes of the slice: x: 4, y: 4, z: 8, core: 2. Of those that a mesh axis runs over, the one named last changes fastest.
Arguments:
- tensor: float32 [2048, 2048, 128], P('row', 'col'), may hold values from -140 to 140
- factor_b0: float32 [2048, 32], P('col'), may hold values from -4 to 4
- factor_c0: float32 [128, 32], replicated, may hold values from -4 to 4
Outputs:
- factor_a: float32 [2048, 32], P('row')
- factor_b: float32 [2048, 32], P('col')
- factor_c: float32 [128, 32], replicated
- weights: float32 [32], replicated
The draws below stay inside these ranges and needn't reach their ends.
All inputs are finite; a program needn't handle non-finite values.
Results may differ from the reference program's by a relative error of at most 0.00013.
Values sent between devices are 32-bit elements; how exact they have to be, the bound alone decides.
A program may use at most 64 MiB of HBM per device.

```python
import math
import jax
import jax.numpy as jnp
from jax import lax

CI = 256
K = 128
R = 32
SWEEPS = 2
I = 2048
J = 2048


def draw_tensor(key, part):
    key = jax.random.fold_in(key, 11)
    key_cells, key_first, key_second, key_third = jax.random.split(key, 4)
    along_i = jnp.arange(I, dtype=jnp.float32) / I
    along_j = jnp.arange(J, dtype=jnp.float32) / J
    along_k = jnp.arange(K, dtype=jnp.float32) / K
    cells = jnp.clip(jax.random.normal(key_cells, (I, J, K), jnp.float32), -4.0, 4.0)
    first = jnp.exp(along_i * math.log(3.0) + jax.random.uniform(key_first, (I,), jnp.float32, 0.0, math.log(10.0))) / 10.0
    second = jnp.exp(along_j * math.log(3.0) + jax.random.uniform(key_second, (J,), jnp.float32, 0.0, math.log(10.0))) / 10.0
    third = jnp.exp(along_k * math.log(3.0) + jax.random.uniform(key_third, (K,), jnp.float32, 0.0, math.log(10.0))) / 10.0
    return cells * first[:, None, None] * second[None, :, None] * third[None, None, :]


def block_levels(stream_key, shape, cuts, smallest, top_value):
    def one(axis_at, shards_of):
        heights = jax.random.uniform(jax.random.fold_in(jax.random.fold_in(stream_key, 6), axis_at), (shards_of,), jnp.float32, smallest / len(cuts), top_value / len(cuts))
        return jnp.repeat(jnp.exp(heights), shape[axis_at] // shards_of).reshape((-1,) + (1,) * (len(shape) - axis_at - 1))

    level = one(*cuts[0])
    for cut in cuts[1:]:
        level = level * one(*cut)
    return level


def centred(rng, dims, width, most, cuts=(), kind=jnp.bfloat16):
    entries = width * jax.random.normal(rng, dims, jnp.float32)
    if cuts:
        entries = entries * block_levels(rng, dims, cuts, -0.22, 0.18)
    return jnp.clip(entries, -most, most).astype(kind)


def setup_inputs(seed: int = 0) -> dict:
    arg_keys = jax.random.split(jax.random.key(seed), 4)
    tensor = draw_tensor(jax.random.fold_in(arg_keys[3], 71), 0)
    factor_b0 = centred(arg_keys[1], (J, R), 1.0, 4.0, ((0, 32),), jnp.float32)
    factor_c0 = centred(arg_keys[2], (K, R), 1.0, 4.0, (), jnp.float32)
    return {"tensor": tensor, "factor_b0": factor_b0, "factor_c0": factor_c0}


EPSILON = 1e-06

def gram_of(factor):
    return jnp.dot(factor.T.astype(jnp.float32), factor.astype(jnp.float32), precision=lax.Precision.HIGHEST, preferred_element_type=jnp.float32)

def solve_rows(mttkrp, system):
    cholesky_low = jnp.linalg.cholesky(system)
    return jax.scipy.linalg.cho_solve((cholesky_low, True), mttkrp.T).T

def normalize(solved, count):
    scales = jnp.sqrt(lax.optimization_barrier(jnp.sum(solved * solved, axis=0)) / count + EPSILON)
    return (solved / scales[None, :], scales)

def reference(tensor, factor_b0, factor_c0):
    row_count = min(CI, 32)
    pieces = tensor.reshape(I // row_count, row_count, J, K)
    factor_b = factor_b0
    factor_c = factor_c0
    gram_b = gram_of(factor_b)
    gram_c = gram_of(factor_c)
    factor_a = jnp.zeros((I, R), jnp.float32)
    weights = jnp.zeros((R,), jnp.float32)
    for sweep_index in range(SWEEPS):

        def rows_a(piece):
            partial_y = jnp.einsum('ijk,jr->irk', piece, factor_b, precision=lax.Precision.HIGHEST)
            return lax.optimization_barrier(jnp.sum(partial_y * factor_c.T[None, :, :], axis=2))
        m_a = lax.map(rows_a, pieces).reshape(I, R)
        factor_a, unused_a = normalize(solve_rows(m_a, gram_b * gram_c), I)
        gram_a = gram_of(factor_a)

        def accumulate(carry, inputs):
            piece, a_piece = inputs
            return (carry + jnp.einsum('ijk,ir->jrk', piece, a_piece, precision=lax.Precision.HIGHEST), None)
        crossed, unused_scan = lax.scan(accumulate, jnp.zeros((J, R, K), jnp.float32), (pieces, factor_a.reshape(I // row_count, row_count, R)))
        m_b = lax.optimization_barrier(jnp.sum(crossed * factor_c.T[None, :, :], axis=2))
        factor_b, unused_b = normalize(solve_rows(m_b, gram_a * gram_c), J)
        gram_b = gram_of(factor_b)
        m_c = jnp.einsum('jrk,jr->kr', crossed, factor_b, precision=lax.Precision.HIGHEST)
        factor_c, weights = normalize(solve_rows(m_c, gram_a * gram_b), K)
        gram_c = gram_of(factor_c)
    return (factor_a, factor_b, factor_c, weights)
```

```python
import functools

import jax
import jax.numpy as jnp
from jax import lax
from jax.experimental import pallas as pl
from jax.experimental.pallas import tpu as pltpu
from jax.sharding import PartitionSpec as P

SWEEPS = 2
EPSILON = 1e-06
F32 = jnp.float32
BF16 = jnp.bfloat16
MESH = pl.DeviceIdType.MESH
NT = (((1,), (1,)), ((), ()))
NN = (((1,), (0,)), ((), ()))
TN = (((0,), (0,)), ((), ()))


def exact(left, right, dims):
    return lax.dot_general(
        left, right, dims, precision=lax.Precision.HIGHEST, preferred_element_type=F32
    )


def fast(left, right, dims):
    return lax.dot_general(left, right, dims, preferred_element_type=F32)


def split(x):
    high = x.astype(BF16)
    return high, (x - high.astype(F32)).astype(BF16)


def pack_square(g):
    return jnp.concatenate([g[8 * q : 8 * q + 8, :] for q in range(4)], axis=1)


def unpack_square(p):
    return jnp.concatenate([p[:, 32 * q : 32 * q + 32] for q in range(4)], axis=0)


def inverse(system):
    row = lax.broadcasted_iota(jnp.int32, (32, 32), 0)
    lane = lax.broadcasted_iota(jnp.int32, (32, 32), 1)
    unit = jnp.where(row == lane, 1.0, 0.0).astype(F32)
    both = jnp.concatenate([system, unit], axis=1)
    parts = [both[8 * q : 8 * q + 8] for q in range(4)]
    sub = lax.broadcasted_iota(jnp.int32, (8, 64), 0)
    out = []
    for k in range(32):
        q, s = divmod(k, 8)
        pivot_row = jnp.broadcast_to(parts[q][s : s + 1, :], (8, 64))
        pivot = jnp.broadcast_to(pivot_row[:, k : k + 1], (8, 64))
        scaled_row = pivot_row * (1.0 / pivot)
        out.append((pivot_row * lax.rsqrt(pivot))[0:1, 32:])
        for t in range(q, 4):
            low = jnp.broadcast_to(parts[t][:, k : k + 1], (8, 64))
            if t == q:
                low = jnp.where(sub > s, low, 0.0)
            parts[t] = parts[t] - low * scaled_row
    w = jnp.concatenate(out, axis=0)
    return exact(w, w, TN)


def scales_of(moments, count):
    row = lax.broadcasted_iota(jnp.int32, (32, 32), 0)
    lane = lax.broadcasted_iota(jnp.int32, (32, 32), 1)
    diagonal = jnp.where(row == lane, moments, 0.0)
    down = jnp.sqrt(jnp.sum(diagonal, axis=1, keepdims=True) / count + EPSILON)
    across = jnp.sqrt(jnp.sum(diagonal, axis=0, keepdims=True) / count + EPSILON)
    return down, moments / (down * across)


def kernel(
    total_i, total_j,
    tensor, b_in, c_in,
    a_out, b_out, c_out, w_out,
    staged, high, low, wide_b, kr, y,
    gram_src, gram_got, ma_src, ma_got, ma_sum, ma_all,
    mom_src, mom_got, mb_src, mb_got,
    mc_src, mc_got, mc_mid, mc_col, mc_sum, mc_all,
    load_sem, gram_sem, ma_sem, maz_sem, mom_sem, mb_sem, mc_sem, mcc_sem, mcr_sem,
):
    row, col = lax.axis_index("row"), lax.axis_index("col")
    z, y_at = col // 4, lax.rem(col, 4)

    barrier = pltpu.get_barrier_semaphore()

    def greet_col(step, carry):
        pl.semaphore_signal(
            barrier, inc=1, device_id=(row, lax.rem(col + step, 32)), device_id_type=MESH
        )
        return carry

    def greet_row(step, carry):
        pl.semaphore_signal(
            barrier, inc=1, device_id=(lax.rem(row + step, 8), col), device_id_type=MESH
        )
        return carry

    lax.fori_loop(1, 32, greet_col, 0)
    lax.fori_loop(1, 8, greet_row, 0)

    def load(j, carry):
        pltpu.make_async_copy(tensor.at[:, j, :], staged.at[j], load_sem.at[j // 8]).start()
        return carry

    lax.fori_loop(0, 64, load, 0)

    sent = []

    def finish(got, count, sem):
        view = got.at[pl.ds(0, count)]
        pltpu.make_async_copy(view, view, sem).wait()

    def to_col(source, got, sems):
        def one(step, carry):
            there = lax.rem(col + step, 32)
            pltpu.make_async_remote_copy(
                src_ref=source, dst_ref=got.at[col], send_sem=sems.at[0], recv_sem=sems.at[1],
                device_id=(row, there), device_id_type=MESH,
            ).start()
            return carry

        lax.fori_loop(1, 32, one, 0)
        sent.append((got, 31, sems.at[0]))

    def to_row(pick, got, sems):
        def one(step, carry):
            there = lax.rem(row + step, 8)
            pltpu.make_async_remote_copy(
                src_ref=pick(there), dst_ref=got.at[row], send_sem=sems.at[0],
                recv_sem=sems.at[1], device_id=(there, col), device_id_type=MESH,
            ).start()
            return carry

        lax.fori_loop(1, 8, one, 0)
        sent.append((got, 7, sems.at[0]))

    def total(got, count):
        acc = got[0]
        for at in range(1, count):
            acc = acc + got[at]
        return acc

    bt = b_in[...]
    ct = c_in[...]
    gram_c = exact(ct, ct, NT)
    gram_src[0] = pack_square(exact(bt, bt, NT))

    def widen(values):
        for j in range(64):
            wide_b[j] = jnp.broadcast_to(values[:, j : j + 1], (32, 128))

    def khatri_rao(third):
        def body(pair, carry):
            h, l = split(
                jnp.concatenate([wide_b[2 * pair] * third, wide_b[2 * pair + 1] * third], axis=1)
            )
            kr[pair, 0:32, :] = h
            kr[pair, 32:64, :] = l
            return carry

        lax.fori_loop(0, 32, body, 0)

    widen(bt)
    khatri_rao(ct)

    pl.semaphore_wait(barrier, 38)
    to_col(gram_src.at[0], gram_got.at[0], gram_sem.at[0])
    gram_got[0, col] = gram_src[0]

    def unpack(group, carry):
        view = staged.at[pl.ds(8 * group, 8)]
        pltpu.make_async_copy(view, view, load_sem.at[group]).wait()
        for at in range(4):
            pair = 4 * group + at
            h, l = split(jnp.concatenate([staged[2 * pair], staged[2 * pair + 1]], axis=1))
            high[pair] = h
            low[pair] = l
        return carry

    lax.fori_loop(0, 8, unpack, 0)

    gram_a = None
    for sweep in range(SWEEPS):
        def product_a(pair, acc):
            p = fast(kr[pair], high[pair], NT)
            q = fast(kr[pair, 0:32, :], low[pair], NT)
            return acc + (p[:32] + p[32:] + q)

        part = lax.fori_loop(0, 32, product_a, jnp.zeros((32, 256), F32), unroll=4)
        for tile in range(8):
            q, half = divmod(tile, 2)
            ma_src[sweep, tile] = part[8 * q : 8 * q + 8, 128 * half : 128 * half + 128]

        def send_tile(step, carry):
            there = lax.rem(col + step, 32)
            pltpu.make_async_remote_copy(
                src_ref=ma_src.at[sweep, there // 4], dst_ref=ma_got.at[sweep, col],
                send_sem=ma_sem.at[sweep, 0], recv_sem=ma_sem.at[sweep, 1],
                device_id=(row, there), device_id_type=MESH,
            ).start()
            return carry

        lax.fori_loop(1, 32, send_tile, 0)
        sent.append((ma_got.at[sweep], 31, ma_sem.at[sweep, 0]))
        ma_got[sweep, col] = ma_src[sweep, z]

        if sweep == 0:
            finish(gram_got.at[0], 31, gram_sem.at[0, 1])
            gram_b = unpack_square(total(gram_got.at[0], 32))
        inverse_a = inverse(gram_b * gram_c)

        finish(ma_got.at[sweep], 31, ma_sem.at[sweep, 1])
        summed = total(ma_got.at[sweep], 32)
        ma_sum[sweep] = summed

        def send_sum(step, carry):
            there = lax.rem(z + step, 8)
            pltpu.make_async_remote_copy(
                src_ref=ma_sum.at[sweep], dst_ref=ma_all.at[sweep, z],
                send_sem=maz_sem.at[sweep, 0], recv_sem=maz_sem.at[sweep, 1],
                device_id=(row, there * 4 + y_at), device_id_type=MESH,
            ).start()
            return carry

        lax.fori_loop(1, 8, send_sum, 0)
        sent.append((ma_all.at[sweep], 7, maz_sem.at[sweep, 0]))
        ma_all[sweep, z] = summed
        finish(ma_all.at[sweep], 7, maz_sem.at[sweep, 1])
        m_a = jnp.concatenate(
            [
                jnp.concatenate([ma_all[sweep, 2 * q], ma_all[sweep, 2 * q + 1]], axis=1)
                for q in range(4)
            ],
            axis=0,
        )
        solved_a = exact(inverse_a, m_a, NN)

        mom_src[sweep] = pack_square(exact(solved_a, solved_a, NT))
        to_row(lambda there: mom_src.at[sweep], mom_got.at[sweep], mom_sem.at[sweep])
        mom_got[sweep, row] = mom_src[sweep]
        a_high, a_low = split(solved_a)
        a_both = jnp.concatenate([a_high, a_low], axis=0)

        def product_y(pair, carry):
            p = fast(a_both, high[pair], NN)
            q = fast(a_high, low[pair], NN)
            y[pair] = p[:32] + p[32:] + q
            return carry

        lax.fori_loop(0, 32, product_y, 0, unroll=4)
        lane = lax.broadcasted_iota(jnp.int32, (32, 64), 1)

        def reduce_y(pair, acc):
            r = y[pair]
            first = jnp.sum(r[:, :128] * ct, axis=1, keepdims=True)
            second = jnp.sum(r[:, 128:] * ct, axis=1, keepdims=True)
            return jnp.where(lane == 2 * pair, first, jnp.where(lane == 2 * pair + 1, second, acc))

        part = lax.fori_loop(0, 32, reduce_y, jnp.zeros((32, 64), F32), unroll=4)
        mb_src[sweep] = jnp.concatenate([part[:16], part[16:]], axis=1)
        to_row(lambda there: mb_src.at[sweep], mb_got.at[sweep], mb_sem.at[sweep])
        mb_got[sweep, row] = mb_src[sweep]

        finish(mom_got.at[sweep], 7, mom_sem.at[sweep, 1])
        scale_a, gram_a = scales_of(unpack_square(total(mom_got.at[sweep], 8)), total_i)
        inverse_b = inverse(gram_a * gram_c)

        finish(mb_got.at[sweep], 7, mb_sem.at[sweep, 1])
        packed = total(mb_got.at[sweep], 8)
        m_b = jnp.concatenate([packed[:, :64], packed[:, 64:]], axis=0) / scale_a
        solved_b = exact(inverse_b, m_b, NN)

        gram_src[sweep + 1] = pack_square(exact(solved_b, solved_b, NT))
        to_col(gram_src.at[sweep + 1], gram_got.at[sweep + 1], gram_sem.at[sweep + 1])
        gram_got[sweep + 1, col] = gram_src[sweep + 1]

        widen(solved_b / scale_a)

        def product_c(pair, acc):
            r = y[pair]
            return acc + r[:, :128] * wide_b[2 * pair] + r[:, 128:] * wide_b[2 * pair + 1]

        part = lax.fori_loop(0, 32, product_c, jnp.zeros((32, 128), F32), unroll=4)
        for piece in range(8):
            mc_src[sweep, piece] = part[4 * piece : 4 * piece + 4]
        to_row(lambda there: mc_src.at[sweep, there], mc_got.at[sweep], mc_sem.at[sweep])
        mc_got[sweep, row] = mc_src[sweep, row]
        finish(mc_got.at[sweep], 7, mc_sem.at[sweep, 1])
        mc_mid[sweep] = total(mc_got.at[sweep], 8)
        to_col(mc_mid.at[sweep], mc_col.at[sweep], mcc_sem.at[sweep])
        mc_col[sweep, col] = mc_mid[sweep]

        finish(gram_got.at[sweep + 1], 31, gram_sem.at[sweep + 1, 1])
        scale_b, gram_b = scales_of(unpack_square(total(gram_got.at[sweep + 1], 32)), total_j)
        inverse_c = inverse(gram_a * gram_b)

        finish(mc_col.at[sweep], 31, mcc_sem.at[sweep, 1])
        mc_sum[sweep] = total(mc_col.at[sweep], 32)
        to_row(lambda there: mc_sum.at[sweep], mc_all.at[sweep], mcr_sem.at[sweep])
        mc_all[sweep, row] = mc_sum[sweep]
        finish(mc_all.at[sweep], 7, mcr_sem.at[sweep, 1])
        m_c = jnp.concatenate([mc_all[sweep, piece] for piece in range(8)], axis=0) / scale_b
        solved_c = exact(inverse_c, m_c, NN)
        weights = jnp.sqrt(
            jnp.sum(solved_c * solved_c, axis=1, keepdims=True) / 128.0 + EPSILON
        )
        ct = solved_c / weights
        if sweep < SWEEPS - 1:
            gram_c = exact(ct, ct, NT)
            khatri_rao(ct * (scale_a / scale_b))
        else:
            a_out[...] = solved_a / scale_a
            b_out[...] = solved_b / scale_b
            c_out[...] = ct
            w_out[...] = weights

    for got, count, sem in sent:
        finish(got, count, sem)


def shards(total_i, total_j, tensor, factor_b0, factor_c0):
    vmem = pl.BlockSpec(memory_space=pltpu.VMEM)
    dma = pltpu.SemaphoreType.DMA
    n = SWEEPS

    def buffer(*shape):
        return pltpu.VMEM(shape, F32)

    a_t, b_t, c_t, w_t = pl.pallas_call(
        functools.partial(kernel, float(total_i), float(total_j)),
        out_shape=[
            jax.ShapeDtypeStruct((32, 256), F32),
            jax.ShapeDtypeStruct((32, 64), F32),
            jax.ShapeDtypeStruct((32, 128), F32),
            jax.ShapeDtypeStruct((32, 1), F32),
        ],
        in_specs=[pl.BlockSpec(memory_space=pl.ANY), vmem, vmem],
        out_specs=[vmem] * 4,
        scratch_shapes=[
            buffer(64, 256, 128),
            pltpu.VMEM((32, 256, 256), BF16),
            pltpu.VMEM((32, 256, 256), BF16),
            buffer(64, 32, 128),
            pltpu.VMEM((32, 64, 256), BF16),
            buffer(32, 32, 256),
            buffer(n + 1, 8, 128), buffer(n + 1, 32, 8, 128),
            buffer(n, 8, 8, 128), buffer(n, 32, 8, 128), buffer(n, 8, 128), buffer(n, 8, 8, 128),
            buffer(n, 8, 128), buffer(n, 8, 8, 128), buffer(n, 16, 128), buffer(n, 8, 16, 128),
            buffer(n, 8, 4, 128), buffer(n, 8, 4, 128), buffer(n, 4, 128),
            buffer(n, 32, 4, 128), buffer(n, 4, 128), buffer(n, 8, 4, 128),
            dma((8,)), dma((n + 1, 2)), dma((n, 2)), dma((n, 2)), dma((n, 2)), dma((n, 2)),
            dma((n, 2)), dma((n, 2)), dma((n, 2)),
        ],
        compiler_params=pltpu.CompilerParams(
            collective_id=0, has_side_effects=True, vmem_limit_bytes=48 * 2**20
        ),
    )(tensor, factor_b0.T, factor_c0.T)
    return a_t.T, b_t.T, c_t.T, w_t[:, 0]


def solution(mesh):
    total_i = 256 * mesh.shape["row"]
    total_j = 64 * mesh.shape["col"]
    return jax.shard_map(
        functools.partial(shards, total_i, total_j),
        mesh=mesh,
        in_specs=(P("row", "col", None), P("col", None), P()),
        out_specs=(P("row", None), P("col", None), P(), P()),
        check_vma=False,
    )
```

```python
import functools

import jax
import jax.numpy as jnp
from jax import lax
from jax.experimental import pallas as pl
from jax.experimental.pallas import tpu as pltpu
from jax.sharding import PartitionSpec as P

SWEEPS = 2
FIRST = 3
EPSILON = 1e-06
F32 = jnp.float32
BF16 = jnp.bfloat16
MESH = pl.DeviceIdType.MESH
NT = (((1,), (1,)), ((), ()))
NN = (((1,), (0,)), ((), ()))
TN = (((0,), (0,)), ((), ()))


def exact(left, right, dims):
    return lax.dot_general(
        left, right, dims, precision=lax.Precision.HIGHEST, preferred_element_type=F32
    )


def fast(left, right, dims):
    return lax.dot_general(left, right, dims, preferred_element_type=F32)


def split(x):
    high = x.astype(BF16)
    return high, (x - high.astype(F32)).astype(BF16)


def far_first(at, ring):
    odd = lax.rem(at, 2)
    return lax.rem(ring // 2 + lax.div(at + 1, 2) * (2 * odd - 1) + ring, ring)


def pack_square(g):
    return jnp.concatenate([g[8 * q : 8 * q + 8, :] for q in range(4)], axis=1)


def unpack_square(p):
    return jnp.concatenate([p[:, 32 * q : 32 * q + 32] for q in range(4)], axis=0)


def lanes(x, at):
    return jnp.broadcast_to(x[:, at : at + 1], (8, 128))


def sublanes(x, at):
    return jnp.broadcast_to(x[at : at + 1, :], (8, 128))


def inverse(system):
    row = lax.broadcasted_iota(jnp.int32, (32, 128), 0)
    lane = lax.broadcasted_iota(jnp.int32, (32, 128), 1)
    unit = jnp.where(lane == row + 32, 1.0, 0.0).astype(F32)
    wide = jnp.concatenate([system, jnp.zeros((32, 96), F32)], axis=1) + unit
    parts = [wide[8 * q : 8 * q + 8] for q in range(4)]
    sub = lax.broadcasted_iota(jnp.int32, (8, 128), 0)
    out = []
    for q in range(4):
        cols = [[lanes(parts[t], 8 * q + c) for t in range(q, 4)] for c in range(8)]
        rows = [sublanes(parts[q], c) for c in range(8)]
        small = [[sublanes(cols[b][0], a) if a >= b else None for b in range(8)] for a in range(8)]
        done = jnp.zeros((8, 128), F32)
        for c in range(8):
            pivot = small[c][c]
            over = 1.0 / pivot
            low = [small[a][c] * over if a > c else None for a in range(8)]
            for a in range(c + 1, 8):
                for b in range(c + 1, a + 1):
                    small[a][b] = small[a][b] - low[a] * small[b][c]
            for a in range(c + 1, 8):
                rows[a] = rows[a] - low[a] * rows[c]
            for t in range(1, 4 - q):
                step = cols[c][t] * over
                for b in range(c + 1, 8):
                    cols[b][t] = cols[b][t] - step * small[b][c]
                parts[q + t] = parts[q + t] - step * rows[c]
            done = jnp.where(sub == c, rows[c] * lax.rsqrt(pivot), done)
        out.append(done)
    w = jnp.concatenate(out, axis=0)[:, 32:64]
    return exact(w, w, TN)


def lane_sums(leaf, first, bits):
    if bits == 0:
        return leaf(first)
    bit = bits - 1
    left = lane_sums(leaf, first, bit)
    right = lane_sums(leaf, first + 2**bit, bit)
    at = lax.broadcasted_iota(jnp.int32, left.shape, 1)
    even = (at & 2**bit) == 0
    moved = pltpu.roll(jnp.where(even, right, left), 128 - 2**bit, 1)
    return jnp.where(even, left, right) + moved


def scales_of(moments, count):
    row = lax.broadcasted_iota(jnp.int32, (32, 32), 0)
    lane = lax.broadcasted_iota(jnp.int32, (32, 32), 1)
    diagonal = jnp.where(row == lane, moments, 0.0)
    down = jnp.sqrt(jnp.sum(diagonal, axis=1, keepdims=True) / count + EPSILON)
    across = jnp.sqrt(jnp.sum(diagonal, axis=0, keepdims=True) / count + EPSILON)
    return down, moments / (down * across)


def kernel(
    total_i, total_j,
    tensor, b_in, c_in,
    a_out, b_out, c_out, w_out,
    b_here, c_here, staged, high, low, wide_b, kr, u, y,
    gram_src, gram_got, ma_src, ma_got, ma_sum, ma_all,
    mom_src, mom_got, mb_src, mb_got,
    mc_src, mc_got, mc_mid, mc_all,
    in_sem, load_sem, gram_sem, ma_sem, maz_sem, mom_sem, mb_sem, mc_sem, mcc_sem,
):
    row, col = lax.axis_index("row"), lax.axis_index("col")
    z, y_at = lax.div(col, 4), lax.rem(col, 4)
    x_at, core = lax.div(row, 2), lax.rem(row, 2)
    place, quarter = 4 * row + y_at, lax.rem(row, 4)
    mine = 2 * y_at + lax.rem(z, 2)
    copy_b = pltpu.make_async_copy(b_in, b_here, in_sem.at[0])
    copy_c = pltpu.make_async_copy(c_in, c_here, in_sem.at[1])
    copy_b.start()
    copy_c.start()

    def load(j, carry):
        pltpu.make_async_copy(tensor.at[:, j, :], staged.at[j], load_sem.at[j // 8]).start()
        return carry

    lax.fori_loop(0, 64, load, 0)

    barrier = pltpu.get_barrier_semaphore()

    ys = [4 * z + lax.rem(y_at + off, 4) for off in (2, 3, 1, 0)]
    y_offs = [lax.rem(y_at + off, 4) for off in (2, 3, 1, 0)]

    def each_col(act):
        def some(step, carry):
            base = 4 * lax.rem(z + far_first(step, 8), 8)
            for off in y_offs:
                act(base + off)
            return carry

        lax.fori_loop(0, 7, some, 0)
        for there in ys[:3]:
            act(there)

    def each_plane(act):
        def some(step, carry):
            base = 2 * lax.rem(x_at + far_first(step, 4), 4)
            for there in ys:
                act(base + 1 - core, there)
                act(base + core, there)
            return carry

        lax.fori_loop(0, 3, some, 0)
        for there in ys[:3]:
            act(2 * x_at + 1 - core, there)
            act(row, there)
        act(2 * x_at + 1 - core, ys[3])

    def greet(there_row, there_col):
        pl.semaphore_signal(
            barrier, inc=1, device_id=(there_row, there_col), device_id_type=MESH
        )

    each_col(lambda there: greet(row, there))
    each_plane(greet)

    sent = []

    def finish(got, count, sem):
        view = got.at[pl.ds(0, count)]
        pltpu.make_async_copy(view, view, sem).wait()

    def send(source, got, slot, device, sems):
        pltpu.make_async_remote_copy(
            src_ref=source, dst_ref=got.at[slot], send_sem=sems.at[0], recv_sem=sems.at[1],
            device_id=device, device_id_type=MESH,
        ).start()

    def to_col(pick, got, sems):
        each_col(lambda there: send(pick(there), got, col, (row, there), sems))
        sent.append((got, 31, sems.at[0]))

    def to_plane(pick, got, sems):
        each_plane(lambda *there: send(pick(there), got, place, there, sems))
        sent.append((got, 31, sems.at[0]))

    def to_row(source, got, sems):
        def one(step, carry):
            send(source, got, row, (lax.rem(row + step, 8), col), sems)
            return carry

        lax.fori_loop(1, 8, one, 0)
        sent.append((got, 7, sems.at[0]))

    def to_tiles(source, got, sems):
        def one(step, carry):
            tile = lax.rem(mine + step, 8)
            there = 4 * (2 * lax.div(z, 2) + lax.rem(tile, 2)) + lax.div(tile, 2)
            send(source, got, mine, (row, there), sems)
            return carry

        lax.fori_loop(1, 8, one, 0)
        sent.append((got, 7, sems.at[0]))

    def to_quarters(source, got, sems):
        rows = [4 * lax.div(row, 4) + lax.rem(quarter + off, 4) for off in (2, 1, 3, 0)]

        def some(step, carry):
            there = 4 * lax.rem(z + far_first(step, 8), 8) + y_at
            for there_row in rows:
                send(source, got, 8 * quarter + z, (there_row, there), sems)
            return carry

        lax.fori_loop(0, 7, some, 0)
        for there_row in rows[:3]:
            send(source, got, 8 * quarter + z, (there_row, col), sems)
        sent.append((got, 31, sems.at[0]))

    def total(got, count):
        acc = got[0]
        for at in range(1, count):
            acc = acc + got[at]
        return acc
    copy_b.wait()
    copy_c.wait()
    bt = b_here[...]
    ct = c_here[...]
    gram_c = exact(ct, ct, NT)
    gram_src[0] = pack_square(exact(bt, bt, NT))

    def widen(values):
        for j in range(64):
            wide_b[j] = jnp.broadcast_to(values[:, j : j + 1], (32, 128))

    def khatri_rao(third):
        def body(pair, carry):
            h, l = split(
                jnp.concatenate([wide_b[2 * pair] * third, wide_b[2 * pair + 1] * third], axis=1)
            )
            kr[pair, 0:32, :] = h
            kr[pair, 32:64, :] = l
            return carry

        lax.fori_loop(0, 32, body, 0)

    widen(bt)
    khatri_rao(ct)

    def product_a(pair, acc):
        p = fast(kr[pair], high[pair], NT)
        q = fast(kr[pair, 0:32, :], low[pair], NT)
        return acc + (p[:32] + p[32:] + q)

    def unpack(group, acc):
        view = staged.at[pl.ds(8 * group, 8)]
        pltpu.make_async_copy(view, view, load_sem.at[group]).wait()
        for at in range(4):
            pair = 4 * group + at
            h, l = split(jnp.concatenate([staged[2 * pair], staged[2 * pair + 1]], axis=1))
            high[pair] = h
            low[pair] = l
            acc = product_a(pair, acc)
        return acc

    gram_a = None
    for sweep in range(SWEEPS):
        if sweep == 0:
            part = lax.fori_loop(0, FIRST, unpack, jnp.zeros((32, 256), F32))
            pl.semaphore_wait(barrier, 62)
            to_col(lambda there: gram_src.at[0], gram_got.at[0], gram_sem.at[0])
            gram_got[0, col] = gram_src[0]
            part = lax.fori_loop(FIRST, 8, unpack, part)
        else:
            part = lax.fori_loop(0, 32, product_a, jnp.zeros((32, 256), F32), unroll=4)
        for tile in range(8):
            q, half = divmod(tile, 2)
            ma_src[sweep, tile] = part[8 * q : 8 * q + 8, 128 * half : 128 * half + 128]

        def tile_of(there):
            tile = 2 * lax.rem(there, 4) + lax.rem(lax.div(there, 4), 2)
            return ma_src.at[sweep, tile]

        to_col(tile_of, ma_got.at[sweep], ma_sem.at[sweep])
        ma_got[sweep, col] = ma_src[sweep, mine]

        c_high, c_low = split(ct)
        none = jnp.zeros((32, 128), BF16)

        def twice(x):
            return jnp.concatenate(
                [jnp.concatenate([x, none], axis=1), jnp.concatenate([none, x], axis=1)], axis=0
            )

        c_high = twice(c_high)
        c_both = jnp.concatenate([c_high, twice(c_low)], axis=0)

        def product_u(pair, carry):
            p = fast(c_both, high[pair], NT)
            q = fast(c_high, low[pair], NT)
            u[pair] = p[:64] + p[64:] + q
            return carry

        lax.fori_loop(0, 32, product_u, 0, unroll=4)
        if sweep == 0:
            finish(gram_got.at[0], 31, gram_sem.at[0, 1])
            gram_b = unpack_square(total(gram_got.at[0], 32))
        inverse_a = inverse(gram_b * gram_c)
        finish(ma_got.at[sweep], 31, ma_sem.at[sweep, 1])
        summed = total(ma_got.at[sweep], 32)
        ma_sum[sweep] = summed

        to_tiles(ma_sum.at[sweep], ma_all.at[sweep], maz_sem.at[sweep])
        ma_all[sweep, mine] = summed
        finish(ma_all.at[sweep], 7, maz_sem.at[sweep, 1])
        m_a = jnp.concatenate(
            [
                jnp.concatenate([ma_all[sweep, 2 * q], ma_all[sweep, 2 * q + 1]], axis=1)
                for q in range(4)
            ],
            axis=0,
        )
        solved_a = exact(inverse_a, m_a, NN)

        mom_src[sweep] = pack_square(exact(solved_a, solved_a, NT))
        to_row(mom_src.at[sweep], mom_got.at[sweep], mom_sem.at[sweep])
        mom_got[sweep, row] = mom_src[sweep]
        def leaf(j):
            pair, at = divmod(j, 2)
            r = u[pair, 32 * at : 32 * at + 32, :] * solved_a
            return r[:, :128] + r[:, 128:]

        part = lane_sums(leaf, 0, 6)
        part = part + pltpu.roll(part, 64, 1)
        lane = lax.broadcasted_iota(jnp.int32, (16, 128), 1)
        mb_src[sweep] = jnp.where(lane < 64, part[:16], part[16:])
        to_row(mb_src.at[sweep], mb_got.at[sweep], mb_sem.at[sweep])
        mb_got[sweep, row] = mb_src[sweep]

        a_high, a_low = split(solved_a)
        a_both = jnp.concatenate([a_high, a_low], axis=0)

        def product_y(pair, carry):
            p = fast(a_both, high[pair], NN)
            q = fast(a_high, low[pair], NN)
            y[pair] = p[:32] + p[32:] + q
            return carry

        lax.fori_loop(0, 32, product_y, 0, unroll=4)
        finish(mom_got.at[sweep], 7, mom_sem.at[sweep, 1])
        scale_a, gram_a = scales_of(unpack_square(total(mom_got.at[sweep], 8)), total_i)
        inverse_b = inverse(gram_a * gram_c)
        finish(mb_got.at[sweep], 7, mb_sem.at[sweep, 1])
        packed = total(mb_got.at[sweep], 8)
        m_b = jnp.concatenate([packed[:, :64], packed[:, 64:]], axis=0) / scale_a
        solved_b = exact(inverse_b, m_b, NN)

        widen(solved_b / scale_a)

        def product_c(pair, acc):
            r = y[pair]
            return acc + r[:, :128] * wide_b[2 * pair] + r[:, 128:] * wide_b[2 * pair + 1]

        part = lax.fori_loop(0, 32, product_c, jnp.zeros((32, 128), F32), unroll=4)
        for piece in range(4):
            mc_src[sweep, piece] = part[8 * piece : 8 * piece + 8]
        to_plane(
            lambda there: mc_src.at[sweep, lax.rem(there[0], 4)], mc_got.at[sweep], mc_sem.at[sweep]
        )
        mc_got[sweep, place] = mc_src[sweep, quarter]
        gram_src[sweep + 1] = pack_square(exact(solved_b, solved_b, NT))
        to_col(lambda there: gram_src.at[sweep + 1], gram_got.at[sweep + 1], gram_sem.at[sweep + 1])
        gram_got[sweep + 1, col] = gram_src[sweep + 1]
        finish(mc_got.at[sweep], 31, mc_sem.at[sweep, 1])
        mc_mid[sweep] = total(mc_got.at[sweep], 32)
        to_quarters(mc_mid.at[sweep], mc_all.at[sweep], mcc_sem.at[sweep])
        mc_all[sweep, 8 * quarter + z] = mc_mid[sweep]

        finish(gram_got.at[sweep + 1], 31, gram_sem.at[sweep + 1, 1])
        scale_b, gram_b = scales_of(unpack_square(total(gram_got.at[sweep + 1], 32)), total_j)
        inverse_c = inverse(gram_a * gram_b)
        finish(mc_all.at[sweep], 31, mcc_sem.at[sweep, 1])
        m_c = jnp.concatenate([total(mc_all.at[sweep, pl.ds(8 * piece, 8)], 8) for piece in range(4)], axis=0) / scale_b
        solved_c = exact(inverse_c, m_c, NN)
        weights = jnp.sqrt(
            jnp.sum(solved_c * solved_c, axis=1, keepdims=True) / 128.0 + EPSILON
        )
        ct = solved_c / weights
        if sweep < SWEEPS - 1:
            gram_c = exact(ct, ct, NT)
            khatri_rao(ct * (scale_a / scale_b))
        else:
            a_out[...] = solved_a / scale_a
            b_out[...] = solved_b / scale_b
            c_out[...] = ct
            at = lax.broadcasted_iota(jnp.int32, (32, 32), 0)
            unit = at == lax.broadcasted_iota(jnp.int32, (32, 32), 1)
            w_out[...] = jnp.sum(jnp.where(unit, weights, 0.0), axis=0, keepdims=True)
    for got, count, sem in sent:
        finish(got, count, sem)


def shards(total_i, total_j, tensor, factor_b0, factor_c0):
    vmem = pl.BlockSpec(memory_space=pltpu.VMEM)
    dma = pltpu.SemaphoreType.DMA
    n = SWEEPS

    def buffer(*shape):
        return pltpu.VMEM(shape, F32)

    results = [
        jax.ShapeDtypeStruct((32, 256), F32),
        jax.ShapeDtypeStruct((32, 64), F32),
        jax.ShapeDtypeStruct((32, 128), F32),
        jax.ShapeDtypeStruct((1, 32), F32),
    ]
    a_t, b_t, c_t, w_t = pl.pallas_call(
        functools.partial(kernel, float(total_i), float(total_j)),
        out_shape=results,
        in_specs=[pl.BlockSpec(memory_space=pltpu.HBM)] * 3,
        out_specs=[vmem] * 4,
        scratch_shapes=[
            buffer(32, 64), buffer(32, 128),
            buffer(64, 256, 128),
            pltpu.VMEM((32, 256, 256), BF16),
            pltpu.VMEM((32, 256, 256), BF16),
            buffer(64, 32, 128),
            pltpu.VMEM((32, 64, 256), BF16),
            buffer(32, 64, 256),
            buffer(32, 32, 256),
            buffer(n + 1, 8, 128), buffer(n + 1, 32, 8, 128),
            buffer(n, 8, 8, 128), buffer(n, 32, 8, 128), buffer(n, 8, 128), buffer(n, 8, 8, 128),
            buffer(n, 8, 128), buffer(n, 8, 8, 128), buffer(n, 16, 128), buffer(n, 8, 16, 128),
            buffer(n, 4, 8, 128), buffer(n, 32, 8, 128), buffer(n, 8, 128),
            buffer(n, 32, 8, 128),
            dma((2,)), dma((8,)), dma((n + 1, 2)), dma((n, 2)), dma((n, 2)), dma((n, 2)), dma((n, 2)),
            dma((n, 2)), dma((n, 2)),
        ],
        compiler_params=pltpu.CompilerParams(
            collective_id=0, has_side_effects=True, vmem_limit_bytes=48 * 2**20
        ),
    )(
        tensor,
        pltpu.with_memory_space_constraint(factor_b0.T, pltpu.HBM),
        pltpu.with_memory_space_constraint(factor_c0.T, pltpu.HBM),
    )
    return a_t.T, b_t.T, c_t.T, w_t[0]


def solution(mesh):
    total_i = 256 * mesh.shape["row"]
    total_j = 64 * mesh.shape["col"]
    return jax.shard_map(
        functools.partial(shards, total_i, total_j),
        mesh=mesh,
        in_specs=(P("row", "col", None), P("col", None), P()),
        out_specs=(P("row", None), P("col", None), P(), P()),
        check_vma=False,
    )
```

```python
import functools

import jax
import jax.numpy as jnp
from jax import lax
from jax.experimental import pallas as pl
from jax.experimental.pallas import tpu as pltpu
from jax.sharding import PartitionSpec as P

SWEEPS = 2
FIRST = 3
TURNS = (20, 26, 8)
EPSILON = 1e-06
F32 = jnp.float32
BF16 = jnp.bfloat16
MESH = pl.DeviceIdType.MESH
NT = (((1,), (1,)), ((), ()))
NN = (((1,), (0,)), ((), ()))
TN = (((0,), (0,)), ((), ()))


def exact(left, right, dims):
    return lax.dot_general(
        left, right, dims, precision=lax.Precision.HIGHEST, preferred_element_type=F32
    )


def fast(left, right, dims):
    return lax.dot_general(left, right, dims, preferred_element_type=F32)


def split(x):
    high = x.astype(BF16)
    return high, (x - high.astype(F32)).astype(BF16)


def far_first(at, ring):
    odd = lax.rem(at, 2)
    return lax.rem(ring // 2 + lax.div(at + 1, 2) * (2 * odd - 1) + ring, ring)


def pack_square(g):
    return jnp.concatenate([g[8 * q : 8 * q + 8, :] for q in range(4)], axis=1)


def unpack_square(p):
    return jnp.concatenate([p[:, 32 * q : 32 * q + 32] for q in range(4)], axis=0)


def lanes(x, at):
    return jnp.broadcast_to(x[:, at : at + 1], (8, 128))


def sublanes(x, at):
    return jnp.broadcast_to(x[at : at + 1, :], (8, 128))


def inverse(system):
    row = lax.broadcasted_iota(jnp.int32, (32, 128), 0)
    lane = lax.broadcasted_iota(jnp.int32, (32, 128), 1)
    unit = jnp.where(lane == row + 32, 1.0, 0.0).astype(F32)
    wide = jnp.concatenate([system, jnp.zeros((32, 96), F32)], axis=1) + unit
    parts = [wide[8 * q : 8 * q + 8] for q in range(4)]
    sub = lax.broadcasted_iota(jnp.int32, (8, 128), 0)
    out = []
    for q in range(4):
        cols = [[lanes(parts[t], 8 * q + c) for t in range(q, 4)] for c in range(8)]
        rows = [sublanes(parts[q], c) for c in range(8)]
        small = [[sublanes(cols[b][0], a) if a >= b else None for b in range(8)] for a in range(8)]
        done = jnp.zeros((8, 128), F32)
        for c in range(8):
            pivot = small[c][c]
            over = 1.0 / pivot
            low = [small[a][c] * over if a > c else None for a in range(8)]
            for a in range(c + 1, 8):
                for b in range(c + 1, a + 1):
                    small[a][b] = small[a][b] - low[a] * small[b][c]
            for a in range(c + 1, 8):
                rows[a] = rows[a] - low[a] * rows[c]
            for t in range(1, 4 - q):
                step = cols[c][t] * over
                for b in range(c + 1, 8):
                    cols[b][t] = cols[b][t] - step * small[b][c]
                parts[q + t] = parts[q + t] - step * rows[c]
            done = jnp.where(sub == c, rows[c] * lax.rsqrt(pivot), done)
        out.append(done)
    w = jnp.concatenate(out, axis=0)[:, 32:64]
    return exact(w, w, TN)


def lane_sums(leaf, first, bits):
    if bits == 0:
        return leaf(first)
    bit = bits - 1
    left = lane_sums(leaf, first, bit)
    right = lane_sums(leaf, first + 2**bit, bit)
    at = lax.broadcasted_iota(jnp.int32, left.shape, 1)
    even = (at & 2**bit) == 0
    moved = pltpu.roll(jnp.where(even, right, left), 128 - 2**bit, 1)
    return jnp.where(even, left, right) + moved


def scales_of(moments, count):
    row = lax.broadcasted_iota(jnp.int32, (32, 32), 0)
    lane = lax.broadcasted_iota(jnp.int32, (32, 32), 1)
    diagonal = jnp.where(row == lane, moments, 0.0)
    down = jnp.sqrt(jnp.sum(diagonal, axis=1, keepdims=True) / count + EPSILON)
    across = jnp.sqrt(jnp.sum(diagonal, axis=0, keepdims=True) / count + EPSILON)
    return down, moments / (down * across)


def kernel(
    total_i, total_j,
    tensor, b_in, c_in,
    a_out, b_out, c_out, w_out,
    b_here, c_here, staged, high, low, wide_b, kr, u, y, turned_high, turned_low, chooser, zed,
    gram_src, gram_got, ma_src, ma_got, ma_sum, ma_all,
    mom_src, mom_got, mb_src, mb_got,
    mc_src, mc_got, mc_mid, mc_all,
    in_sem, load_sem, gram_sem, ma_sem, maz_sem, mom_sem, mb_sem, mc_sem, mcc_sem,
):
    row, col = lax.axis_index("row"), lax.axis_index("col")
    z, y_at = lax.div(col, 4), lax.rem(col, 4)
    x_at, core = lax.div(row, 2), lax.rem(row, 2)
    place, quarter = 4 * row + y_at, lax.rem(row, 4)
    mine = 2 * y_at + lax.rem(z, 2)
    copy_b = pltpu.make_async_copy(b_in, b_here, in_sem.at[0])
    copy_c = pltpu.make_async_copy(c_in, c_here, in_sem.at[1])
    copy_b.start()
    copy_c.start()

    def load(j, carry):
        pltpu.make_async_copy(tensor.at[:, j, :], staged.at[j], load_sem.at[j // 8]).start()
        return carry

    lax.fori_loop(0, 16, load, 0)

    barrier = pltpu.get_barrier_semaphore()

    ys = [4 * z + lax.rem(y_at + off, 4) for off in (2, 3, 1, 0)]
    y_offs = [lax.rem(y_at + off, 4) for off in (2, 3, 1, 0)]

    def each_col(act):
        def some(step, carry):
            base = 4 * lax.rem(z + far_first(step, 8), 8)
            for off in y_offs:
                act(base + off)
            return carry

        lax.fori_loop(0, 7, some, 0)
        for there in ys[:3]:
            act(there)

    def each_plane(act):
        def some(step, carry):
            base = 2 * lax.rem(x_at + far_first(step, 4), 4)
            for there in ys:
                act(base + 1 - core, there)
                act(base + core, there)
            return carry

        lax.fori_loop(0, 3, some, 0)
        for there in ys[:3]:
            act(2 * x_at + 1 - core, there)
            act(row, there)
        act(2 * x_at + 1 - core, ys[3])

    def greet(there_row, there_col):
        pl.semaphore_signal(
            barrier, inc=1, device_id=(there_row, there_col), device_id_type=MESH
        )

    each_col(lambda there: greet(row, there))
    each_plane(greet)
    lax.fori_loop(16, 64, load, 0)

    sent = []

    def finish(got, count, sem):
        view = got.at[pl.ds(0, count)]
        pltpu.make_async_copy(view, view, sem).wait()

    def send(source, got, slot, device, sems):
        pltpu.make_async_remote_copy(
            src_ref=source, dst_ref=got.at[slot], send_sem=sems.at[0], recv_sem=sems.at[1],
            device_id=device, device_id_type=MESH,
        ).start()

    def to_col(pick, got, sems):
        each_col(lambda there: send(pick(there), got, col, (row, there), sems))
        sent.append((got, 31, sems.at[0]))

    def to_plane(pick, got, sems):
        each_plane(lambda *there: send(pick(there), got, place, there, sems))
        sent.append((got, 31, sems.at[0]))

    def to_row(source, got, sems):
        def one(step, carry):
            send(source, got, row, (lax.rem(row + step, 8), col), sems)
            return carry

        lax.fori_loop(1, 8, one, 0)
        sent.append((got, 7, sems.at[0]))

    def to_tiles(source, got, sems):
        def one(step, carry):
            tile = lax.rem(mine + step, 8)
            there = 4 * (2 * lax.div(z, 2) + lax.rem(tile, 2)) + lax.div(tile, 2)
            send(source, got, mine, (row, there), sems)
            return carry

        lax.fori_loop(1, 8, one, 0)
        sent.append((got, 7, sems.at[0]))

    def to_quarters(source, got, sems):
        rows = [4 * lax.div(row, 4) + lax.rem(quarter + off, 4) for off in (2, 1, 3, 0)]

        def some(step, carry):
            there = 4 * lax.rem(z + far_first(step, 8), 8) + y_at
            for there_row in rows:
                send(source, got, 8 * quarter + z, (there_row, there), sems)
            return carry

        lax.fori_loop(0, 7, some, 0)
        for there_row in rows[:3]:
            send(source, got, 8 * quarter + z, (there_row, col), sems)
        sent.append((got, 31, sems.at[0]))

    def total(got, count):
        acc = got[0]
        for at in range(1, count):
            acc = acc + got[at]
        return acc
    copy_b.wait()
    copy_c.wait()
    bt = b_here[...]
    ct = c_here[...]
    gram_c = exact(ct, ct, NT)
    gram_src[0] = pack_square(exact(bt, bt, NT))

    def widen(values):
        for j in range(64):
            wide_b[j] = jnp.broadcast_to(values[:, j : j + 1], (32, 128))

    def khatri_rao(third):
        def body(pair, carry):
            h, l = split(
                jnp.concatenate([wide_b[2 * pair] * third, wide_b[2 * pair + 1] * third], axis=1)
            )
            kr[pair, 0:32, :] = h
            kr[pair, 32:64, :] = l
            return carry

        lax.fori_loop(0, 32, body, 0)

    widen(bt)
    khatri_rao(ct)

    def product_a(pair, acc):
        p = fast(kr[pair], high[pair], NT)
        q = fast(kr[pair, 0:32, :], low[pair], NT)
        return acc + (p[:32] + p[32:] + q)

    def turn(pair, carry):
        first, second = staged[2 * pair].T, staged[2 * pair + 1].T
        at = pl.multiple_of(16 * lax.rem(pair, 16), 16)
        for k8 in range(16):
            rows = slice(8 * k8, 8 * k8 + 8)
            h, l = split(jnp.concatenate([first[rows], second[rows]], axis=0))
            turned_high[k8, lax.div(pair, 16), pl.ds(at, 16), :] = h
            turned_low[k8, lax.div(pair, 16), pl.ds(at, 16), :] = l
        return carry

    def spread(values):
        lane = lax.broadcasted_iota(jnp.int32, (32, 256), 1)
        row = lax.broadcasted_iota(jnp.int32, (32, 256), 0)
        repeat = jnp.where(lax.div(lane, 8) == row, 1.0, 0.0).astype(F32)
        for half in range(2):
            wide = exact(values[:, 32 * half : 32 * half + 32], repeat, NN)
            for k in range(8):
                h, l = split(jnp.where(lax.rem(lane, 8) == k, wide, 0.0))
                chooser[half, 32 * k : 32 * k + 32, :] = h
                chooser[half, 256 + 32 * k : 256 + 32 * k + 32, :] = l

    def product_z(k8, carry):
        acc = None
        for half in range(2):
            p = fast(chooser[half], turned_high[k8, half], NN)
            q = fast(chooser[half, 0:256, :], turned_low[k8, half], NN)
            r = p[:256] + p[256:] + q
            acc = r if acc is None else acc + r
        zed[k8] = acc
        return carry

    def contract_z(third):
        acc = jnp.zeros((32, 256), F32)
        for k in range(128):
            k8, at = divmod(k, 8)
            factor = jnp.broadcast_to(third[:, k : k + 1], (32, 128))
            r = zed[k8, 32 * at : 32 * at + 32, :]
            acc = acc + r * jnp.concatenate([factor, factor], axis=1)
        return acc

    def unpack(group, acc):
        view = staged.at[pl.ds(8 * group, 8)]
        pltpu.make_async_copy(view, view, load_sem.at[group]).wait()
        for at in range(4):
            pair = 4 * group + at
            h, l = split(jnp.concatenate([staged[2 * pair], staged[2 * pair + 1]], axis=1))
            high[pair] = h
            low[pair] = l
            acc = product_a(pair, acc)
        return acc

    gram_a = None
    for sweep in range(SWEEPS):
        if sweep == 0:
            part = lax.fori_loop(0, FIRST, unpack, jnp.zeros((32, 256), F32))
            pl.semaphore_wait(barrier, 62)
            to_col(lambda there: gram_src.at[0], gram_got.at[0], gram_sem.at[0])
            gram_got[0, col] = gram_src[0]
            part = lax.fori_loop(FIRST, 8, unpack, part)
        else:
            part = contract_z(ct * (scale_a / scale_b))
        for tile in range(8):
            q, half = divmod(tile, 2)
            ma_src[sweep, tile] = part[8 * q : 8 * q + 8, 128 * half : 128 * half + 128]

        def tile_of(there):
            tile = 2 * lax.rem(there, 4) + lax.rem(lax.div(there, 4), 2)
            return ma_src.at[sweep, tile]

        to_col(tile_of, ma_got.at[sweep], ma_sem.at[sweep])
        ma_got[sweep, col] = ma_src[sweep, mine]

        c_high, c_low = split(ct)
        none = jnp.zeros((32, 128), BF16)

        def twice(x):
            return jnp.concatenate(
                [jnp.concatenate([x, none], axis=1), jnp.concatenate([none, x], axis=1)], axis=0
            )

        c_high = twice(c_high)
        c_both = jnp.concatenate([c_high, twice(c_low)], axis=0)

        def product_u(pair, carry):
            p = fast(c_both, high[pair], NT)
            q = fast(c_high, low[pair], NT)
            u[pair] = p[:64] + p[64:] + q
            return carry

        lax.fori_loop(0, 32, product_u, 0, unroll=4)
        if sweep == 0:
            finish(gram_got.at[0], 31, gram_sem.at[0, 1])
            gram_b = unpack_square(total(gram_got.at[0], 32))
        inverse_a = inverse(gram_b * gram_c)
        finish(ma_got.at[sweep], 31, ma_sem.at[sweep, 1])
        summed = total(ma_got.at[sweep], 32)
        ma_sum[sweep] = summed

        to_tiles(ma_sum.at[sweep], ma_all.at[sweep], maz_sem.at[sweep])
        ma_all[sweep, mine] = summed
        if sweep == 0:
            lax.fori_loop(0, TURNS[0], turn, 0, unroll=2)
        finish(ma_all.at[sweep], 7, maz_sem.at[sweep, 1])
        m_a = jnp.concatenate(
            [
                jnp.concatenate([ma_all[sweep, 2 * q], ma_all[sweep, 2 * q + 1]], axis=1)
                for q in range(4)
            ],
            axis=0,
        )
        solved_a = exact(inverse_a, m_a, NN)

        mom_src[sweep] = pack_square(exact(solved_a, solved_a, NT))
        to_row(mom_src.at[sweep], mom_got.at[sweep], mom_sem.at[sweep])
        mom_got[sweep, row] = mom_src[sweep]
        def leaf(j):
            pair, at = divmod(j, 2)
            r = u[pair, 32 * at : 32 * at + 32, :] * solved_a
            return r[:, :128] + r[:, 128:]

        part = lane_sums(leaf, 0, 6)
        part = part + pltpu.roll(part, 64, 1)
        lane = lax.broadcasted_iota(jnp.int32, (16, 128), 1)
        mb_src[sweep] = jnp.where(lane < 64, part[:16], part[16:])
        to_row(mb_src.at[sweep], mb_got.at[sweep], mb_sem.at[sweep])
        mb_got[sweep, row] = mb_src[sweep]

        a_high, a_low = split(solved_a)
        a_both = jnp.concatenate([a_high, a_low], axis=0)

        def product_y(pair, carry):
            p = fast(a_both, high[pair], NN)
            q = fast(a_high, low[pair], NN)
            y[pair] = p[:32] + p[32:] + q
            return carry

        lax.fori_loop(0, 32, product_y, 0, unroll=4)
        if sweep == 0:
            lax.fori_loop(TURNS[0], TURNS[1], turn, 0, unroll=2)
        finish(mom_got.at[sweep], 7, mom_sem.at[sweep, 1])
        scale_a, gram_a = scales_of(unpack_square(total(mom_got.at[sweep], 8)), total_i)
        inverse_b = inverse(gram_a * gram_c)
        finish(mb_got.at[sweep], 7, mb_sem.at[sweep, 1])
        packed = total(mb_got.at[sweep], 8)
        m_b = jnp.concatenate([packed[:, :64], packed[:, 64:]], axis=0) / scale_a
        solved_b = exact(inverse_b, m_b, NN)

        widen(solved_b / scale_a)

        def product_c(pair, acc):
            r = y[pair]
            return acc + r[:, :128] * wide_b[2 * pair] + r[:, 128:] * wide_b[2 * pair + 1]

        part = lax.fori_loop(0, 32, product_c, jnp.zeros((32, 128), F32), unroll=4)
        for piece in range(4):
            mc_src[sweep, piece] = part[8 * piece : 8 * piece + 8]
        to_plane(
            lambda there: mc_src.at[sweep, lax.rem(there[0], 4)], mc_got.at[sweep], mc_sem.at[sweep]
        )
        mc_got[sweep, place] = mc_src[sweep, quarter]
        gram_src[sweep + 1] = pack_square(exact(solved_b, solved_b, NT))
        to_col(lambda there: gram_src.at[sweep + 1], gram_got.at[sweep + 1], gram_sem.at[sweep + 1])
        gram_got[sweep + 1, col] = gram_src[sweep + 1]
        if sweep == 0:
            lax.fori_loop(TURNS[1], 32, turn, 0, unroll=2)
            spread(solved_b / scale_a)
            lax.fori_loop(0, TURNS[2], product_z, 0, unroll=2)
        finish(mc_got.at[sweep], 31, mc_sem.at[sweep, 1])
        mc_mid[sweep] = total(mc_got.at[sweep], 32)
        to_quarters(mc_mid.at[sweep], mc_all.at[sweep], mcc_sem.at[sweep])
        mc_all[sweep, 8 * quarter + z] = mc_mid[sweep]

        if sweep == 0:
            lax.fori_loop(TURNS[2], 16, product_z, 0, unroll=2)
        finish(gram_got.at[sweep + 1], 31, gram_sem.at[sweep + 1, 1])
        scale_b, gram_b = scales_of(unpack_square(total(gram_got.at[sweep + 1], 32)), total_j)
        inverse_c = inverse(gram_a * gram_b)
        finish(mc_all.at[sweep], 31, mcc_sem.at[sweep, 1])
        m_c = jnp.concatenate([total(mc_all.at[sweep, pl.ds(8 * piece, 8)], 8) for piece in range(4)], axis=0) / scale_b
        solved_c = exact(inverse_c, m_c, NN)
        weights = jnp.sqrt(
            jnp.sum(solved_c * solved_c, axis=1, keepdims=True) / 128.0 + EPSILON
        )
        ct = solved_c / weights
        if sweep < SWEEPS - 1:
            gram_c = exact(ct, ct, NT)
        else:
            a_out[...] = solved_a / scale_a
            b_out[...] = solved_b / scale_b
            c_out[...] = ct
            at = lax.broadcasted_iota(jnp.int32, (32, 32), 0)
            unit = at == lax.broadcasted_iota(jnp.int32, (32, 32), 1)
            w_out[...] = jnp.sum(jnp.where(unit, weights, 0.0), axis=0, keepdims=True)
    for got, count, sem in sent:
        finish(got, count, sem)


def shards(total_i, total_j, tensor, factor_b0, factor_c0):
    vmem = pl.BlockSpec(memory_space=pltpu.VMEM)
    dma = pltpu.SemaphoreType.DMA
    n = SWEEPS

    def buffer(*shape):
        return pltpu.VMEM(shape, F32)

    results = [
        jax.ShapeDtypeStruct((32, 256), F32),
        jax.ShapeDtypeStruct((32, 64), F32),
        jax.ShapeDtypeStruct((32, 128), F32),
        jax.ShapeDtypeStruct((1, 32), F32),
    ]
    a_t, b_t, c_t, w_t = pl.pallas_call(
        functools.partial(kernel, float(total_i), float(total_j)),
        out_shape=results,
        in_specs=[pl.BlockSpec(memory_space=pltpu.HBM)] * 3,
        out_specs=[vmem] * 4,
        scratch_shapes=[
            buffer(32, 64), buffer(32, 128),
            buffer(64, 256, 128),
            pltpu.VMEM((32, 256, 256), BF16),
            pltpu.VMEM((32, 256, 256), BF16),
            buffer(64, 32, 128),
            pltpu.VMEM((32, 64, 256), BF16),
            buffer(32, 64, 256),
            buffer(32, 32, 256),
            pltpu.VMEM((16, 2, 256, 256), BF16),
            pltpu.VMEM((16, 2, 256, 256), BF16),
            pltpu.VMEM((2, 512, 256), BF16),
            buffer(16, 256, 256),
            buffer(n + 1, 8, 128), buffer(n + 1, 32, 8, 128),
            buffer(n, 8, 8, 128), buffer(n, 32, 8, 128), buffer(n, 8, 128), buffer(n, 8, 8, 128),
            buffer(n, 8, 128), buffer(n, 8, 8, 128), buffer(n, 16, 128), buffer(n, 8, 16, 128),
            buffer(n, 4, 8, 128), buffer(n, 32, 8, 128), buffer(n, 8, 128),
            buffer(n, 32, 8, 128),
            dma((2,)), dma((8,)), dma((n + 1, 2)), dma((n, 2)), dma((n, 2)), dma((n, 2)), dma((n, 2)),
            dma((n, 2)), dma((n, 2)),
        ],
        compiler_params=pltpu.CompilerParams(
            collective_id=0, has_side_effects=True, vmem_limit_bytes=48 * 2**20
        ),
    )(
        tensor,
        pltpu.with_memory_space_constraint(factor_b0.T, pltpu.HBM),
        pltpu.with_memory_space_constraint(factor_c0.T, pltpu.HBM),
    )
    return a_t.T, b_t.T, c_t.T, w_t[0]


def solution(mesh):
    total_i = 256 * mesh.shape["row"]
    total_j = 64 * mesh.shape["col"]
    return jax.shard_map(
        functools.partial(shards, total_i, total_j),
        mesh=mesh,
        in_specs=(P("row", "col", None), P("col", None), P()),
        out_specs=(P("row", None), P("col", None), P(), P()),
        check_vma=False,
    )
```

```python
import functools

import jax
import jax.numpy as jnp
from jax import lax
from jax.experimental import pallas as pl
from jax.experimental.pallas import tpu as pltpu
from jax.sharding import PartitionSpec as P

SWEEPS = 2
FIRST = 4
TURNS = (20, 26, 8)
EPSILON = 1e-06
F32 = jnp.float32
BF16 = jnp.bfloat16
MESH = pl.DeviceIdType.MESH
NT = (((1,), (1,)), ((), ()))
NN = (((1,), (0,)), ((), ()))
TN = (((0,), (0,)), ((), ()))


def exact(left, right, dims):
    return lax.dot_general(
        left, right, dims, precision=lax.Precision.HIGHEST, preferred_element_type=F32
    )


def fast(left, right, dims):
    return lax.dot_general(left, right, dims, preferred_element_type=F32)


def split(x):
    high = x.astype(BF16)
    return high, (x - high.astype(F32)).astype(BF16)


def far_first(at, ring):
    odd = lax.rem(at, 2)
    return lax.rem(ring // 2 + lax.div(at + 1, 2) * (2 * odd - 1) + ring, ring)


def pack_square(g):
    return jnp.concatenate([g[8 * q : 8 * q + 8, :] for q in range(4)], axis=1)


def unpack_square(p):
    return jnp.concatenate([p[:, 32 * q : 32 * q + 32] for q in range(4)], axis=0)


def lanes(x, at):
    return jnp.broadcast_to(x[:, at : at + 1], (8, 128))


def sublanes(x, at):
    return jnp.broadcast_to(x[at : at + 1, :], (8, 128))


def inverse(system):
    row = lax.broadcasted_iota(jnp.int32, (32, 128), 0)
    lane = lax.broadcasted_iota(jnp.int32, (32, 128), 1)
    unit = jnp.where(lane == row + 32, 1.0, 0.0).astype(F32)
    wide = jnp.concatenate([system, jnp.zeros((32, 96), F32)], axis=1) + unit
    parts = [wide[8 * q : 8 * q + 8] for q in range(4)]
    sub = lax.broadcasted_iota(jnp.int32, (8, 128), 0)
    out = []
    for q in range(4):
        cols = [[lanes(parts[t], 8 * q + c) for t in range(q, 4)] for c in range(8)]
        rows = [sublanes(parts[q], c) for c in range(8)]
        small = [[sublanes(cols[b][0], a) if a >= b else None for b in range(8)] for a in range(8)]
        done = jnp.zeros((8, 128), F32)
        for c in range(8):
            pivot = small[c][c]
            over = 1.0 / pivot
            low = [small[a][c] * over if a > c else None for a in range(8)]
            for a in range(c + 1, 8):
                for b in range(c + 1, a + 1):
                    small[a][b] = small[a][b] - low[a] * small[b][c]
            for a in range(c + 1, 8):
                rows[a] = rows[a] - low[a] * rows[c]
            for t in range(1, 4 - q):
                step = cols[c][t] * over
                for b in range(c + 1, 8):
                    cols[b][t] = cols[b][t] - step * small[b][c]
                parts[q + t] = parts[q + t] - step * rows[c]
            done = jnp.where(sub == c, rows[c] * lax.rsqrt(pivot), done)
        out.append(done)
    w = jnp.concatenate(out, axis=0)[:, 32:64]
    return exact(w, w, TN)


def lane_sums(leaf, first, bits):
    if bits == 0:
        return leaf(first)
    bit = bits - 1
    left = lane_sums(leaf, first, bit)
    right = lane_sums(leaf, first + 2**bit, bit)
    at = lax.broadcasted_iota(jnp.int32, left.shape, 1)
    even = (at & 2**bit) == 0
    moved = pltpu.roll(jnp.where(even, right, left), 128 - 2**bit, 1)
    return jnp.where(even, left, right) + moved


def scales_of(moments, count):
    row = lax.broadcasted_iota(jnp.int32, (32, 32), 0)
    lane = lax.broadcasted_iota(jnp.int32, (32, 32), 1)
    diagonal = jnp.where(row == lane, moments, 0.0)
    down = jnp.sqrt(jnp.sum(diagonal, axis=1, keepdims=True) / count + EPSILON)
    across = jnp.sqrt(jnp.sum(diagonal, axis=0, keepdims=True) / count + EPSILON)
    return down, moments / (down * across)


def kernel(
    total_i, total_j,
    tensor, b_in, c_in,
    out,
    b_here, c_here, staged, high, low, u, y, turned_high, turned_low, chooser, zed,
    gram_src, gram_got, ma_src, ma_got, ma_sum, ma_all,
    mom_src, mom_got, mb_src, mb_got,
    mc_src, mc_got, mc_mid, mc_all,
    in_sem, load_sem, gram_sem, ma_sem, maz_sem, mom_sem, mb_sem, mc_sem, mcc_sem,
):
    row, col = lax.axis_index("row"), lax.axis_index("col")
    z, y_at = lax.div(col, 4), lax.rem(col, 4)
    x_at, core = lax.div(row, 2), lax.rem(row, 2)
    place, quarter = 4 * row + y_at, lax.rem(row, 4)
    mine = 2 * y_at + lax.rem(z, 2)
    copy_b = pltpu.make_async_copy(b_in, b_here, in_sem.at[0])
    copy_c = pltpu.make_async_copy(c_in, c_here, in_sem.at[1])
    copy_b.start()
    copy_c.start()

    def load(j, carry):
        pltpu.make_async_copy(tensor.at[:, j, :], staged.at[j], load_sem.at[j // 8]).start()
        return carry

    lax.fori_loop(0, 16, load, 0)

    barrier = pltpu.get_barrier_semaphore()

    ys = [4 * z + lax.rem(y_at + off, 4) for off in (2, 3, 1, 0)]
    y_offs = [lax.rem(y_at + off, 4) for off in (2, 3, 1, 0)]

    def each_col(act):
        def some(step, carry):
            base = 4 * lax.rem(z + far_first(step, 8), 8)
            for off in y_offs:
                act(base + off)
            return carry

        lax.fori_loop(0, 7, some, 0)
        for there in ys[:3]:
            act(there)

    def each_plane(act):
        def some(step, carry):
            base = 2 * lax.rem(x_at + far_first(step, 4), 4)
            for there in ys:
                act(base + 1 - core, there)
                act(base + core, there)
            return carry

        lax.fori_loop(0, 3, some, 0)
        for there in ys[:3]:
            act(2 * x_at + 1 - core, there)
            act(row, there)
        act(2 * x_at + 1 - core, ys[3])

    def greet(there_row, there_col):
        pl.semaphore_signal(
            barrier, inc=1, device_id=(there_row, there_col), device_id_type=MESH
        )

    each_col(lambda there: greet(row, there))
    each_plane(greet)
    lax.fori_loop(16, 64, load, 0)

    sent = []

    def finish(got, count, sem):
        view = got.at[pl.ds(0, count)]
        pltpu.make_async_copy(view, view, sem).wait()

    def send(source, got, slot, device, sems):
        pltpu.make_async_remote_copy(
            src_ref=source, dst_ref=got.at[slot], send_sem=sems.at[0], recv_sem=sems.at[1],
            device_id=device, device_id_type=MESH,
        ).start()

    def to_col(pick, got, sems):
        each_col(lambda there: send(pick(there), got, col, (row, there), sems))
        sent.append((got, 31, sems.at[0]))

    def to_plane(pick, got, sems):
        each_plane(lambda *there: send(pick(there), got, place, there, sems))
        sent.append((got, 31, sems.at[0]))

    def to_row(source, got, sems):
        def one(step, carry):
            send(source, got, row, (lax.rem(row + step, 8), col), sems)
            return carry

        lax.fori_loop(1, 8, one, 0)
        sent.append((got, 7, sems.at[0]))

    def to_tiles(source, got, sems):
        def one(step, carry):
            tile = lax.rem(mine + step, 8)
            there = 4 * (2 * lax.div(z, 2) + lax.rem(tile, 2)) + lax.div(tile, 2)
            send(source, got, mine, (row, there), sems)
            return carry

        lax.fori_loop(1, 8, one, 0)
        sent.append((got, 7, sems.at[0]))

    def to_quarters(source, got, sems):
        rows = [4 * lax.div(row, 4) + lax.rem(quarter + off, 4) for off in (2, 1, 3, 0)]

        def some(step, carry):
            there = 4 * lax.rem(z + far_first(step, 8), 8) + y_at
            for there_row in rows:
                send(source, got, 8 * quarter + z, (there_row, there), sems)
            return carry

        lax.fori_loop(0, 7, some, 0)
        for there_row in rows[:3]:
            send(source, got, 8 * quarter + z, (there_row, col), sems)
        sent.append((got, 31, sems.at[0]))

    def total(got, count):
        acc = got[0]
        for at in range(1, count):
            acc = acc + got[at]
        return acc
    copy_b.wait()
    copy_c.wait()
    bt = b_here[...]
    ct = c_here[...]
    def turn(pair, carry):
        first, second = staged[2 * pair].T, staged[2 * pair + 1].T
        at = pl.multiple_of(16 * lax.rem(pair, 16), 16)
        for k8 in range(16):
            rows = slice(8 * k8, 8 * k8 + 8)
            h, l = split(jnp.concatenate([first[rows], second[rows]], axis=0))
            turned_high[k8, lax.div(pair, 16), pl.ds(at, 16), :] = h
            turned_low[k8, lax.div(pair, 16), pl.ds(at, 16), :] = l
        return carry

    def spread(values):
        lane = lax.broadcasted_iota(jnp.int32, (32, 256), 1)
        row = lax.broadcasted_iota(jnp.int32, (32, 256), 0)
        repeat = jnp.where(lax.div(lane, 8) == row, 1.0, 0.0).astype(F32)
        for half in range(2):
            wide = exact(values[:, 32 * half : 32 * half + 32], repeat, NN)
            for k in range(8):
                h, l = split(jnp.where(lax.rem(lane, 8) == k, wide, 0.0))
                chooser[half, 32 * k : 32 * k + 32, :] = h
                chooser[half, 256 + 32 * k : 256 + 32 * k + 32, :] = l

    def product_z(k8, carry):
        acc = None
        for half in range(2):
            p = fast(chooser[half], turned_high[k8, half], NN)
            q = fast(chooser[half, 0:256, :], turned_low[k8, half], NN)
            r = p[:256] + p[256:] + q
            acc = r if acc is None else acc + r
        zed[k8] = acc
        return carry

    def contract_z(third):
        acc = jnp.zeros((32, 256), F32)
        for k in range(128):
            k8, at = divmod(k, 8)
            factor = jnp.broadcast_to(third[:, k : k + 1], (32, 128))
            r = zed[k8, 32 * at : 32 * at + 32, :]
            acc = acc + r * jnp.concatenate([factor, factor], axis=1)
        return acc

    def first_product(groups, acc):
        for group in groups:
            view = staged.at[pl.ds(8 * group, 8)]
            pltpu.make_async_copy(view, view, load_sem.at[group]).wait()
            for pair in range(4 * group, 4 * group + 4):
                h, l = split(jnp.concatenate([staged[2 * pair], staged[2 * pair + 1]], axis=1))
                high[pair] = h
                low[pair] = l
                first = jnp.broadcast_to(bt[:, 2 * pair : 2 * pair + 1], (32, 128))
                second = jnp.broadcast_to(bt[:, 2 * pair + 1 : 2 * pair + 2], (32, 128))
                rows_h, rows_l = split(jnp.concatenate([first * ct, second * ct], axis=1))
                p = fast(jnp.concatenate([rows_h, rows_l], axis=0), h, NT)
                acc = acc + (p[:32] + p[32:] + fast(rows_h, l, NT))
        return acc

    gram_a = None
    for sweep in range(SWEEPS):
        if sweep == 0:
            part = first_product(range(FIRST), jnp.zeros((32, 256), F32))
            gram_src[0] = pack_square(exact(bt, bt, NT))
            pl.semaphore_wait(barrier, 62)
            to_col(lambda there: gram_src.at[0], gram_got.at[0], gram_sem.at[0])
            gram_got[0, col] = gram_src[0]
            part = first_product(range(FIRST, 8), part)
        else:
            part = contract_z(ct * (scale_a / scale_b))
        for tile in range(8):
            q, half = divmod(tile, 2)
            ma_src[sweep, tile] = part[8 * q : 8 * q + 8, 128 * half : 128 * half + 128]

        def tile_of(there):
            tile = 2 * lax.rem(there, 4) + lax.rem(lax.div(there, 4), 2)
            return ma_src.at[sweep, tile]

        to_col(tile_of, ma_got.at[sweep], ma_sem.at[sweep])
        ma_got[sweep, col] = ma_src[sweep, mine]

        if sweep == 0:
            gram_c = exact(ct, ct, NT)
        c_high, c_low = split(ct)
        none = jnp.zeros((32, 128), BF16)

        def twice(x):
            return jnp.concatenate(
                [jnp.concatenate([x, none], axis=1), jnp.concatenate([none, x], axis=1)], axis=0
            )

        c_high = twice(c_high)
        c_both = jnp.concatenate([c_high, twice(c_low)], axis=0)

        def product_u(pair, carry):
            p = fast(c_both, high[pair], NT)
            q = fast(c_high, low[pair], NT)
            u[pair] = p[:64] + p[64:] + q
            return carry

        lax.fori_loop(0, 32, product_u, 0, unroll=4)
        if sweep == 0:
            finish(gram_got.at[0], 31, gram_sem.at[0, 1])
            gram_b = unpack_square(total(gram_got.at[0], 32))
        inverse_a = inverse(gram_b * gram_c)
        finish(ma_got.at[sweep], 31, ma_sem.at[sweep, 1])
        summed = total(ma_got.at[sweep], 32)
        ma_sum[sweep] = summed

        to_tiles(ma_sum.at[sweep], ma_all.at[sweep], maz_sem.at[sweep])
        ma_all[sweep, mine] = summed
        if sweep == 0:
            lax.fori_loop(0, TURNS[0], turn, 0, unroll=2)
        finish(ma_all.at[sweep], 7, maz_sem.at[sweep, 1])
        m_a = jnp.concatenate(
            [
                jnp.concatenate([ma_all[sweep, 2 * q], ma_all[sweep, 2 * q + 1]], axis=1)
                for q in range(4)
            ],
            axis=0,
        )
        solved_a = exact(inverse_a, m_a, NN)

        mom_src[sweep] = pack_square(exact(solved_a, solved_a, NT))
        to_row(mom_src.at[sweep], mom_got.at[sweep], mom_sem.at[sweep])
        mom_got[sweep, row] = mom_src[sweep]
        def leaf(j):
            pair, at = divmod(j, 2)
            r = u[pair, 32 * at : 32 * at + 32, :] * solved_a
            return r[:, :128] + r[:, 128:]

        part = lane_sums(leaf, 0, 6)
        part = part + pltpu.roll(part, 64, 1)
        lane = lax.broadcasted_iota(jnp.int32, (16, 128), 1)
        mb_src[sweep] = jnp.where(lane < 64, part[:16], part[16:])
        to_row(mb_src.at[sweep], mb_got.at[sweep], mb_sem.at[sweep])
        mb_got[sweep, row] = mb_src[sweep]

        a_high, a_low = split(solved_a)
        a_both = jnp.concatenate([a_high, a_low], axis=0)

        def product_y(pair, carry):
            p = fast(a_both, high[pair], NN)
            q = fast(a_high, low[pair], NN)
            y[pair] = p[:32] + p[32:] + q
            return carry

        lax.fori_loop(0, 32, product_y, 0, unroll=4)
        if sweep == 0:
            lax.fori_loop(TURNS[0], TURNS[1], turn, 0, unroll=2)
        finish(mom_got.at[sweep], 7, mom_sem.at[sweep, 1])
        scale_a, gram_a = scales_of(unpack_square(total(mom_got.at[sweep], 8)), total_i)
        inverse_b = inverse(gram_a * gram_c)
        finish(mb_got.at[sweep], 7, mb_sem.at[sweep, 1])
        packed = total(mb_got.at[sweep], 8)
        m_b = jnp.concatenate([packed[:, :64], packed[:, 64:]], axis=0) / scale_a
        solved_b = exact(inverse_b, m_b, NN)

        rescaled_b = solved_b / scale_a
        part = jnp.zeros((32, 128), F32)
        for j in range(64):
            r = y[j // 2, :, 128 * (j % 2) : 128 * (j % 2) + 128]
            part = part + r * jnp.broadcast_to(rescaled_b[:, j : j + 1], (32, 128))
        for piece in range(4):
            mc_src[sweep, piece] = part[8 * piece : 8 * piece + 8]
        to_plane(
            lambda there: mc_src.at[sweep, lax.rem(there[0], 4)], mc_got.at[sweep], mc_sem.at[sweep]
        )
        mc_got[sweep, place] = mc_src[sweep, quarter]
        gram_src[sweep + 1] = pack_square(exact(solved_b, solved_b, NT))
        to_col(lambda there: gram_src.at[sweep + 1], gram_got.at[sweep + 1], gram_sem.at[sweep + 1])
        gram_got[sweep + 1, col] = gram_src[sweep + 1]
        if sweep == 0:
            lax.fori_loop(TURNS[1], 32, turn, 0, unroll=2)
            spread(rescaled_b)
            lax.fori_loop(0, TURNS[2], product_z, 0, unroll=2)
        finish(mc_got.at[sweep], 31, mc_sem.at[sweep, 1])
        mc_mid[sweep] = total(mc_got.at[sweep], 32)
        to_quarters(mc_mid.at[sweep], mc_all.at[sweep], mcc_sem.at[sweep])
        mc_all[sweep, 8 * quarter + z] = mc_mid[sweep]

        if sweep == 0:
            lax.fori_loop(TURNS[2], 16, product_z, 0, unroll=2)
        finish(gram_got.at[sweep + 1], 31, gram_sem.at[sweep + 1, 1])
        scale_b, gram_b = scales_of(unpack_square(total(gram_got.at[sweep + 1], 32)), total_j)
        inverse_c = inverse(gram_a * gram_b)
        finish(mc_all.at[sweep], 31, mcc_sem.at[sweep, 1])
        m_c = jnp.concatenate([total(mc_all.at[sweep, pl.ds(8 * piece, 8)], 8) for piece in range(4)], axis=0) / scale_b
        solved_c = exact(inverse_c, m_c, NN)
        weights = jnp.sqrt(
            jnp.sum(solved_c * solved_c, axis=1, keepdims=True) / 128.0 + EPSILON
        )
        ct = solved_c / weights
        if sweep < SWEEPS - 1:
            gram_c = exact(ct, ct, NT)
        else:
            at = lax.broadcasted_iota(jnp.int32, (32, 32), 0)
            unit = at == lax.broadcasted_iota(jnp.int32, (32, 32), 1)
            across = jnp.sum(jnp.where(unit, weights, 0.0), axis=0, keepdims=True)
            out[:, 0:256] = solved_a / scale_a
            out[:, 256:320] = solved_b / scale_b
            out[:, 320:352] = jnp.broadcast_to(across, (32, 32))
            out[:, 352:384] = jnp.zeros((32, 32), F32)
            out[:, 384:512] = ct
    for got, count, sem in sent:
        finish(got, count, sem)


def deliver(held, a_out, b_out, c_out, w_out):
    a_out[...] = held[:, 0:256]
    b_out[...] = held[:, 256:320]
    c_out[...] = held[:, 384:512]
    w_out[...] = held[0:1, 320:352]


def shards(total_i, total_j, tensor, factor_b0, factor_c0):
    vmem = pl.BlockSpec(memory_space=pltpu.VMEM)
    dma = pltpu.SemaphoreType.DMA
    n = SWEEPS

    def buffer(*shape):
        return pltpu.VMEM(shape, F32)

    held = pl.pallas_call(
        functools.partial(kernel, float(total_i), float(total_j)),
        out_shape=jax.ShapeDtypeStruct((32, 512), F32),
        in_specs=[pl.BlockSpec(memory_space=pltpu.HBM)] * 3,
        out_specs=vmem,
        scratch_shapes=[
            buffer(32, 64), buffer(32, 128),
            buffer(64, 256, 128),
            pltpu.VMEM((32, 256, 256), BF16),
            pltpu.VMEM((32, 256, 256), BF16),
            buffer(32, 64, 256),
            buffer(32, 32, 256),
            pltpu.VMEM((16, 2, 256, 256), BF16),
            pltpu.VMEM((16, 2, 256, 256), BF16),
            pltpu.VMEM((2, 512, 256), BF16),
            buffer(16, 256, 256),
            buffer(n + 1, 8, 128), buffer(n + 1, 32, 8, 128),
            buffer(n, 8, 8, 128), buffer(n, 32, 8, 128), buffer(n, 8, 128), buffer(n, 8, 8, 128),
            buffer(n, 8, 128), buffer(n, 8, 8, 128), buffer(n, 16, 128), buffer(n, 8, 16, 128),
            buffer(n, 4, 8, 128), buffer(n, 32, 8, 128), buffer(n, 8, 128),
            buffer(n, 32, 8, 128),
            dma((2,)), dma((8,)), dma((n + 1, 2)), dma((n, 2)), dma((n, 2)), dma((n, 2)), dma((n, 2)),
            dma((n, 2)), dma((n, 2)),
        ],
        compiler_params=pltpu.CompilerParams(
            collective_id=0, has_side_effects=True, vmem_limit_bytes=48 * 2**20
        ),
    )(
        tensor,
        pltpu.with_memory_space_constraint(factor_b0.T, pltpu.HBM),
        pltpu.with_memory_space_constraint(factor_c0.T, pltpu.HBM),
    )
    a_t, b_t, c_t, w_t = pl.pallas_call(
        deliver,
        out_shape=[
            jax.ShapeDtypeStruct((32, 256), F32),
            jax.ShapeDtypeStruct((32, 64), F32),
            jax.ShapeDtypeStruct((32, 128), F32),
            jax.ShapeDtypeStruct((1, 32), F32),
        ],
        in_specs=[vmem],
        out_specs=[vmem] * 4,
    )(held)
    return a_t.T, b_t.T, c_t.T, w_t[0]


def solution(mesh):
    total_i = 256 * mesh.shape["row"]
    total_j = 64 * mesh.shape["col"]
    return jax.shard_map(
        functools.partial(shards, total_i, total_j),
        mesh=mesh,
        in_specs=(P("row", "col", None), P("col", None), P()),
        out_specs=(P("row", None), P("col", None), P(), P()),
        check_vma=False,
    )
```

```python
import functools

import jax
import jax.numpy as jnp
from jax import lax
from jax.experimental import pallas as pl
from jax.experimental.pallas import tpu as pltpu
from jax.sharding import PartitionSpec as P

SWEEPS = 2
FIRST = 4
TURNS = (20, 26, 8)
EPSILON = 1e-06
F32 = jnp.float32
BF16 = jnp.bfloat16
MESH = pl.DeviceIdType.MESH
NT = (((1,), (1,)), ((), ()))
NN = (((1,), (0,)), ((), ()))
TN = (((0,), (0,)), ((), ()))


def exact(left, right, dims):
    return lax.dot_general(
        left, right, dims, precision=lax.Precision.HIGHEST, preferred_element_type=F32
    )


def fast(left, right, dims):
    return lax.dot_general(left, right, dims, preferred_element_type=F32)


def split(x):
    high = x.astype(BF16)
    return high, (x - high.astype(F32)).astype(BF16)


def far_first(at, ring):
    odd = lax.rem(at, 2)
    return lax.rem(ring // 2 + lax.div(at + 1, 2) * (2 * odd - 1) + ring, ring)


def pack_square(g):
    return jnp.concatenate([g[8 * q : 8 * q + 8, :] for q in range(4)], axis=1)


def unpack_square(p):
    return jnp.concatenate([p[:, 32 * q : 32 * q + 32] for q in range(4)], axis=0)


def lanes(x, at):
    return jnp.broadcast_to(x[:, at : at + 1], (8, 128))


def sublanes(x, at):
    return jnp.broadcast_to(x[at : at + 1, :], (8, 128))


def inverse(system, spread_cols, spread_rows):
    row = lax.broadcasted_iota(jnp.int32, (32, 128), 0)
    lane = lax.broadcasted_iota(jnp.int32, (32, 128), 1)
    unit = jnp.where(lane == row + 32, 1.0, 0.0).astype(F32)
    wide = jnp.concatenate([system, jnp.zeros((32, 96), F32)], axis=1) + unit
    parts = [wide[8 * q : 8 * q + 8] for q in range(4)]
    sub = lax.broadcasted_iota(jnp.int32, (8, 128), 0)
    out = []
    for q in range(4):
        cols = [[lanes(parts[t], 8 * q + c) for t in range(q, 4)] for c in range(8)]
        spread_rows[q] = parts[q]
        for b in range(8):
            spread_cols[q, b] = cols[b][0]
        rows = [jnp.broadcast_to(spread_rows[q, c : c + 1, :], (8, 128)) for c in range(8)]
        small = [
            [jnp.broadcast_to(spread_cols[q, b, a : a + 1, :], (8, 128)) if a >= b else None for b in range(8)] for a in range(8)
        ]
        done = jnp.zeros((8, 128), F32)
        for c in range(8):
            pivot = small[c][c]
            over = 1.0 / pivot
            low = [small[a][c] * over if a > c else None for a in range(8)]
            for a in range(c + 1, 8):
                for b in range(c + 1, a + 1):
                    small[a][b] = small[a][b] - low[a] * small[b][c]
            for a in range(c + 1, 8):
                rows[a] = rows[a] - low[a] * rows[c]
            for t in range(1, 4 - q):
                step = cols[c][t] * over
                for b in range(c + 1, 8):
                    cols[b][t] = cols[b][t] - step * small[b][c]
                parts[q + t] = parts[q + t] - step * rows[c]
            done = jnp.where(sub == c, rows[c] * lax.rsqrt(pivot), done)
        out.append(done)
    w = jnp.concatenate(out, axis=0)[:, 32:64]
    return exact(w, w, TN)


def lane_sums(leaf, first, bits):
    if bits == 0:
        return leaf(first)
    bit = bits - 1
    left = lane_sums(leaf, first, bit)
    right = lane_sums(leaf, first + 2**bit, bit)
    at = lax.broadcasted_iota(jnp.int32, left.shape, 1)
    even = (at & 2**bit) == 0
    moved = pltpu.roll(jnp.where(even, right, left), 128 - 2**bit, 1)
    return jnp.where(even, left, right) + moved


def scales_of(moments, count):
    row = lax.broadcasted_iota(jnp.int32, (32, 32), 0)
    lane = lax.broadcasted_iota(jnp.int32, (32, 32), 1)
    diagonal = jnp.where(row == lane, moments, 0.0)
    down = jnp.sqrt(jnp.sum(diagonal, axis=1, keepdims=True) / count + EPSILON)
    across = jnp.sqrt(jnp.sum(diagonal, axis=0, keepdims=True) / count + EPSILON)
    return down, moments / (down * across)


def kernel(
    total_i, total_j,
    tensor, b_in, c_in,
    out,
    b_here, c_here, staged, high, low, u, y, turned_high, turned_low, chooser, zed, spread_cols, spread_rows,
    gram_src, gram_got, ma_src, ma_got, ma_sum, ma_all,
    mom_src, mom_got, mb_src, mb_got,
    mc_src, mc_got, mc_mid, mc_all,
    in_sem, load_sem, gram_sem, ma_sem, maz_sem, mom_sem, mb_sem, mc_sem, mcc_sem,
):
    row, col = lax.axis_index("row"), lax.axis_index("col")
    z, y_at = lax.div(col, 4), lax.rem(col, 4)
    x_at, core = lax.div(row, 2), lax.rem(row, 2)
    place, quarter = 4 * row + y_at, lax.rem(row, 4)
    mine = 2 * y_at + lax.rem(z, 2)
    copy_b = pltpu.make_async_copy(b_in, b_here, in_sem.at[0])
    copy_c = pltpu.make_async_copy(c_in, c_here, in_sem.at[1])
    copy_b.start()
    copy_c.start()

    def load(j, carry):
        pltpu.make_async_copy(tensor.at[:, j, :], staged.at[j], load_sem.at[j // 8]).start()
        return carry

    lax.fori_loop(0, 16, load, 0)

    barrier = pltpu.get_barrier_semaphore()

    ys = [4 * z + lax.rem(y_at + off, 4) for off in (2, 3, 1, 0)]
    y_offs = [lax.rem(y_at + off, 4) for off in (2, 3, 1, 0)]

    def each_col(act):
        for z_off in (4, 5, 3, 6, 2, 7, 1):
            base = 4 * lax.rem(z + z_off, 8)
            for off in y_offs:
                act(base + off)
        for there in ys[:3]:
            act(there)

    def each_plane(act):
        def some(step, carry):
            base = 2 * lax.rem(x_at + far_first(step, 4), 4)
            for there in ys:
                act(base + 1 - core, there)
                act(base + core, there)
            return carry

        lax.fori_loop(0, 3, some, 0)
        for there in ys[:3]:
            act(2 * x_at + 1 - core, there)
            act(row, there)
        act(2 * x_at + 1 - core, ys[3])

    def greet(there_row, there_col):
        pl.semaphore_signal(
            barrier, inc=1, device_id=(there_row, there_col), device_id_type=MESH
        )

    each_col(lambda there: greet(row, there))
    each_plane(greet)
    lax.fori_loop(16, 64, load, 0)

    sent = []

    def finish(got, count, sem):
        view = got.at[pl.ds(0, count)]
        pltpu.make_async_copy(view, view, sem).wait()

    def send(source, got, slot, device, sems):
        pltpu.make_async_remote_copy(
            src_ref=source, dst_ref=got.at[slot], send_sem=sems.at[0], recv_sem=sems.at[1],
            device_id=device, device_id_type=MESH,
        ).start()

    def to_col(pick, got, sems):
        each_col(lambda there: send(pick(there), got, col, (row, there), sems))
        sent.append((got, 31, sems.at[0]))

    def to_plane(pick, got, sems):
        each_plane(lambda *there: send(pick(there), got, place, there, sems))
        sent.append((got, 31, sems.at[0]))

    def to_row(source, got, sems):
        def one(step, carry):
            send(source, got, row, (lax.rem(row + step, 8), col), sems)
            return carry

        lax.fori_loop(1, 8, one, 0)
        sent.append((got, 7, sems.at[0]))

    def to_tiles(source, got, sems):
        def one(step, carry):
            tile = lax.rem(mine + step, 8)
            there = 4 * (2 * lax.div(z, 2) + lax.rem(tile, 2)) + lax.div(tile, 2)
            send(source, got, mine, (row, there), sems)
            return carry

        lax.fori_loop(1, 8, one, 0)
        sent.append((got, 7, sems.at[0]))

    def to_quarters(source, got, sems):
        rows = [4 * lax.div(row, 4) + lax.rem(quarter + off, 4) for off in (2, 1, 3, 0)]

        def some(step, carry):
            there = 4 * lax.rem(z + far_first(step, 8), 8) + y_at
            for there_row in rows:
                send(source, got, 8 * quarter + z, (there_row, there), sems)
            return carry

        lax.fori_loop(0, 7, some, 0)
        for there_row in rows[:3]:
            send(source, got, 8 * quarter + z, (there_row, col), sems)
        sent.append((got, 31, sems.at[0]))

    def total(got, count):
        acc = got[0]
        for at in range(1, count):
            acc = acc + got[at]
        return acc
    copy_b.wait()
    copy_c.wait()
    bt = b_here[...]
    ct = c_here[...]
    def turn(pair, carry):
        first, second = staged[2 * pair].T, staged[2 * pair + 1].T
        at = pl.multiple_of(16 * lax.rem(pair, 16), 16)
        for k8 in range(16):
            rows = slice(8 * k8, 8 * k8 + 8)
            h, l = split(jnp.concatenate([first[rows], second[rows]], axis=0))
            turned_high[k8, lax.div(pair, 16), pl.ds(at, 16), :] = h
            turned_low[k8, lax.div(pair, 16), pl.ds(at, 16), :] = l
        return carry

    def spread(values):
        lane = lax.broadcasted_iota(jnp.int32, (32, 256), 1)
        row = lax.broadcasted_iota(jnp.int32, (32, 256), 0)
        repeat = jnp.where(lax.div(lane, 8) == row, 1.0, 0.0).astype(F32)
        for half in range(2):
            wide = exact(values[:, 32 * half : 32 * half + 32], repeat, NN)
            for k in range(8):
                h, l = split(jnp.where(lax.rem(lane, 8) == k, wide, 0.0))
                chooser[half, 32 * k : 32 * k + 32, :] = h
                chooser[half, 256 + 32 * k : 256 + 32 * k + 32, :] = l

    def product_z(k8, carry):
        acc = None
        for half in range(2):
            p = fast(chooser[half], turned_high[k8, half], NN)
            q = fast(chooser[half, 0:256, :], turned_low[k8, half], NN)
            r = p[:256] + p[256:] + q
            acc = r if acc is None else acc + r
        zed[k8] = acc
        return carry

    def contract_z(third):
        acc = jnp.zeros((32, 256), F32)
        for k in range(128):
            k8, at = divmod(k, 8)
            factor = jnp.broadcast_to(third[:, k : k + 1], (32, 128))
            r = zed[k8, 32 * at : 32 * at + 32, :]
            acc = acc + r * jnp.concatenate([factor, factor], axis=1)
        return acc

    def first_product(groups, acc):
        for group in groups:
            view = staged.at[pl.ds(8 * group, 8)]
            pltpu.make_async_copy(view, view, load_sem.at[group]).wait()
            for pair in range(4 * group, 4 * group + 4):
                h, l = split(jnp.concatenate([staged[2 * pair], staged[2 * pair + 1]], axis=1))
                high[pair] = h
                low[pair] = l
                first = jnp.broadcast_to(bt[:, 2 * pair : 2 * pair + 1], (32, 128))
                second = jnp.broadcast_to(bt[:, 2 * pair + 1 : 2 * pair + 2], (32, 128))
                rows_h, rows_l = split(jnp.concatenate([first * ct, second * ct], axis=1))
                p = fast(jnp.concatenate([rows_h, rows_l], axis=0), h, NT)
                acc = acc + (p[:32] + p[32:] + fast(rows_h, l, NT))
        return acc

    gram_a = None
    for sweep in range(SWEEPS):
        if sweep == 0:
            part = first_product(range(FIRST), jnp.zeros((32, 256), F32))
            gram_src[0] = pack_square(exact(bt, bt, NT))
            pl.semaphore_wait(barrier, 62)
            to_col(lambda there: gram_src.at[0], gram_got.at[0], gram_sem.at[0])
            gram_got[0, col] = gram_src[0]
            part = first_product(range(FIRST, 8), part)
        else:
            part = contract_z(ct * (scale_a / scale_b))
        for tile in range(8):
            q, half = divmod(tile, 2)
            ma_src[sweep, tile] = part[8 * q : 8 * q + 8, 128 * half : 128 * half + 128]

        def tile_of(there):
            tile = 2 * lax.rem(there, 4) + lax.rem(lax.div(there, 4), 2)
            return ma_src.at[sweep, tile]

        to_col(tile_of, ma_got.at[sweep], ma_sem.at[sweep])
        ma_got[sweep, col] = ma_src[sweep, mine]

        if sweep == 0:
            gram_c = exact(ct, ct, NT)
        c_high, c_low = split(ct)
        none = jnp.zeros((32, 128), BF16)

        def twice(x):
            return jnp.concatenate(
                [jnp.concatenate([x, none], axis=1), jnp.concatenate([none, x], axis=1)], axis=0
            )

        c_high = twice(c_high)
        c_both = jnp.concatenate([c_high, twice(c_low)], axis=0)

        def product_u(pair, carry):
            p = fast(c_both, high[pair], NT)
            q = fast(c_high, low[pair], NT)
            u[pair] = p[:64] + p[64:] + q
            return carry

        lax.fori_loop(0, 32, product_u, 0, unroll=4)
        if sweep == 0:
            finish(gram_got.at[0], 31, gram_sem.at[0, 1])
            gram_b = unpack_square(total(gram_got.at[0], 32))
        inverse_a = inverse(gram_b * gram_c, spread_cols, spread_rows)
        finish(ma_got.at[sweep], 31, ma_sem.at[sweep, 1])
        summed = total(ma_got.at[sweep], 32)
        ma_sum[sweep] = summed

        to_tiles(ma_sum.at[sweep], ma_all.at[sweep], maz_sem.at[sweep])
        ma_all[sweep, mine] = summed
        if sweep == 0:
            lax.fori_loop(0, TURNS[0], turn, 0, unroll=2)
        finish(ma_all.at[sweep], 7, maz_sem.at[sweep, 1])
        m_a = jnp.concatenate(
            [
                jnp.concatenate([ma_all[sweep, 2 * q], ma_all[sweep, 2 * q + 1]], axis=1)
                for q in range(4)
            ],
            axis=0,
        )
        solved_a = exact(inverse_a, m_a, NN)

        mom_src[sweep] = pack_square(exact(solved_a, solved_a, NT))
        to_row(mom_src.at[sweep], mom_got.at[sweep], mom_sem.at[sweep])
        mom_got[sweep, row] = mom_src[sweep]
        def leaf(j):
            pair, at = divmod(j, 2)
            r = u[pair, 32 * at : 32 * at + 32, :] * solved_a
            return r[:, :128] + r[:, 128:]

        part = lane_sums(leaf, 0, 6)
        part = part + pltpu.roll(part, 64, 1)
        lane = lax.broadcasted_iota(jnp.int32, (16, 128), 1)
        mb_src[sweep] = jnp.where(lane < 64, part[:16], part[16:])
        to_row(mb_src.at[sweep], mb_got.at[sweep], mb_sem.at[sweep])
        mb_got[sweep, row] = mb_src[sweep]

        a_high, a_low = split(solved_a)
        a_both = jnp.concatenate([a_high, a_low], axis=0)

        def product_y(pair, carry):
            p = fast(a_both, high[pair], NN)
            q = fast(a_high, low[pair], NN)
            y[pair] = p[:32] + p[32:] + q
            return carry

        lax.fori_loop(0, 32, product_y, 0, unroll=4)
        if sweep == 0:
            lax.fori_loop(TURNS[0], TURNS[1], turn, 0, unroll=2)
        finish(mom_got.at[sweep], 7, mom_sem.at[sweep, 1])
        scale_a, gram_a = scales_of(unpack_square(total(mom_got.at[sweep], 8)), total_i)
        inverse_b = inverse(gram_a * gram_c, spread_cols, spread_rows)
        finish(mb_got.at[sweep], 7, mb_sem.at[sweep, 1])
        packed = total(mb_got.at[sweep], 8)
        m_b = jnp.concatenate([packed[:, :64], packed[:, 64:]], axis=0) / scale_a
        solved_b = exact(inverse_b, m_b, NN)

        rescaled_b = solved_b / scale_a
        part = jnp.zeros((32, 128), F32)
        for j in range(64):
            r = y[j // 2, :, 128 * (j % 2) : 128 * (j % 2) + 128]
            part = part + r * jnp.broadcast_to(rescaled_b[:, j : j + 1], (32, 128))
        for piece in range(4):
            mc_src[sweep, piece] = part[8 * piece : 8 * piece + 8]
        to_plane(
            lambda there: mc_src.at[sweep, lax.rem(there[0], 4)], mc_got.at[sweep], mc_sem.at[sweep]
        )
        mc_got[sweep, place] = mc_src[sweep, quarter]
        gram_src[sweep + 1] = pack_square(exact(solved_b, solved_b, NT))
        to_col(lambda there: gram_src.at[sweep + 1], gram_got.at[sweep + 1], gram_sem.at[sweep + 1])
        gram_got[sweep + 1, col] = gram_src[sweep + 1]
        if sweep == 0:
            lax.fori_loop(TURNS[1], 32, turn, 0, unroll=2)
            spread(rescaled_b)
            lax.fori_loop(0, TURNS[2], product_z, 0, unroll=2)
        finish(mc_got.at[sweep], 31, mc_sem.at[sweep, 1])
        mc_mid[sweep] = total(mc_got.at[sweep], 32)
        to_quarters(mc_mid.at[sweep], mc_all.at[sweep], mcc_sem.at[sweep])
        mc_all[sweep, 8 * quarter + z] = mc_mid[sweep]

        if sweep == 0:
            lax.fori_loop(TURNS[2], 16, product_z, 0, unroll=2)
        finish(gram_got.at[sweep + 1], 31, gram_sem.at[sweep + 1, 1])
        scale_b, gram_b = scales_of(unpack_square(total(gram_got.at[sweep + 1], 32)), total_j)
        inverse_c = inverse(gram_a * gram_b, spread_cols, spread_rows)
        finish(mc_all.at[sweep], 31, mcc_sem.at[sweep, 1])
        m_c = jnp.concatenate([total(mc_all.at[sweep, pl.ds(8 * piece, 8)], 8) for piece in range(4)], axis=0) / scale_b
        solved_c = exact(inverse_c, m_c, NN)
        weights = jnp.sqrt(
            jnp.sum(solved_c * solved_c, axis=1, keepdims=True) / 128.0 + EPSILON
        )
        ct = solved_c / weights
        if sweep < SWEEPS - 1:
            gram_c = exact(ct, ct, NT)
        else:
            at = lax.broadcasted_iota(jnp.int32, (32, 32), 0)
            unit = at == lax.broadcasted_iota(jnp.int32, (32, 32), 1)
            across = jnp.sum(jnp.where(unit, weights, 0.0), axis=0, keepdims=True)
            out[:, 0:256] = solved_a / scale_a
            out[:, 256:320] = solved_b / scale_b
            out[:, 320:352] = jnp.broadcast_to(across, (32, 32))
            out[:, 352:384] = jnp.zeros((32, 32), F32)
            out[:, 384:512] = ct
    for got, count, sem in sent:
        finish(got, count, sem)


def deliver(held, a_out, b_out, c_out, w_out):
    a_out[...] = held[:, 0:256]
    b_out[...] = held[:, 256:320]
    c_out[...] = held[:, 384:512]
    w_out[...] = held[0:1, 320:352]


def shards(total_i, total_j, tensor, factor_b0, factor_c0):
    vmem = pl.BlockSpec(memory_space=pltpu.VMEM)
    dma = pltpu.SemaphoreType.DMA
    n = SWEEPS

    def buffer(*shape):
        return pltpu.VMEM(shape, F32)

    held = pl.pallas_call(
        functools.partial(kernel, float(total_i), float(total_j)),
        out_shape=jax.ShapeDtypeStruct((32, 512), F32),
        in_specs=[pl.BlockSpec(memory_space=pltpu.HBM)] * 3,
        out_specs=vmem,
        scratch_shapes=[
            buffer(32, 64), buffer(32, 128),
            buffer(64, 256, 128),
            pltpu.VMEM((32, 256, 256), BF16),
            pltpu.VMEM((32, 256, 256), BF16),
            buffer(32, 64, 256),
            buffer(32, 32, 256),
            pltpu.VMEM((16, 2, 256, 256), BF16),
            pltpu.VMEM((16, 2, 256, 256), BF16),
            pltpu.VMEM((2, 512, 256), BF16),
            buffer(16, 256, 256),
            buffer(4, 8, 8, 128), buffer(4, 8, 128),
            buffer(n + 1, 8, 128), buffer(n + 1, 32, 8, 128),
            buffer(n, 8, 8, 128), buffer(n, 32, 8, 128), buffer(n, 8, 128), buffer(n, 8, 8, 128),
            buffer(n, 8, 128), buffer(n, 8, 8, 128), buffer(n, 16, 128), buffer(n, 8, 16, 128),
            buffer(n, 4, 8, 128), buffer(n, 32, 8, 128), buffer(n, 8, 128),
            buffer(n, 32, 8, 128),
            dma((2,)), dma((8,)), dma((n + 1, 2)), dma((n, 2)), dma((n, 2)), dma((n, 2)), dma((n, 2)),
            dma((n, 2)), dma((n, 2)),
        ],
        compiler_params=pltpu.CompilerParams(
            collective_id=0, has_side_effects=True, vmem_limit_bytes=48 * 2**20
        ),
    )(
        tensor,
        pltpu.with_memory_space_constraint(factor_b0.T, pltpu.HBM),
        pltpu.with_memory_space_constraint(factor_c0.T, pltpu.HBM),
    )
    a_t, b_t, c_t, w_t = pl.pallas_call(
        deliver,
        out_shape=[
            jax.ShapeDtypeStruct((32, 256), F32),
            jax.ShapeDtypeStruct((32, 64), F32),
            jax.ShapeDtypeStruct((32, 128), F32),
            jax.ShapeDtypeStruct((1, 32), F32),
        ],
        in_specs=[vmem],
        out_specs=[vmem] * 4,
    )(held)
    return a_t.T, b_t.T, c_t.T, w_t[0]


def solution(mesh):
    total_i = 256 * mesh.shape["row"]
    total_j = 64 * mesh.shape["col"]
    return jax.shard_map(
        functools.partial(shards, total_i, total_j),
        mesh=mesh,
        in_specs=(P("row", "col", None), P("col", None), P()),
        out_specs=(P("row", None), P("col", None), P(), P()),
        check_vma=False,
    )
```
